128 devices in a mesh: pulse: 8 (over z, y_lo), tile: 16 (over y_hi, x, core).
Axes of the slice: x: 4, y: 4 (y_hi: 2, y_lo: 2; y = y_hi * 2 + y_lo), z: 4, core: 2. Of those that a mesh axis runs over, the one named last changes fastest.
Arguments:
- raw: bfloat16 [2, 512, 2048], P(None, ('pulse', 'tile')), may hold values from -6 to 6
- filt: bfloat16 [2, 1024, 2048], replicated, may hold values from -0.125 to 0.125
- range_off: int32 [512], P(('pulse', 'tile')), may hold values from 0 to 1024
- fine: int32 [512], P(('pulse', 'tile')), may hold values from 0 to 3
- dop: int32 [512], P(('pulse', 'tile')), may hold values from 0 to 1023
- pulse_order: int32 [128, 4], P(('pulse', 'tile')), may hold values from 0 to 3, each once within a row
- band_idx: int32 [16, 512], P(None, ('pulse', 'tile')), may hold values from 0 to 1023
Outputs:
- image: bfloat16 [2, 1024, 65536], P(None, 'pulse', 'tile')
The draws below stay inside these ranges and needn't reach their ends.
Inputs may be any that keep to these rules, and one draw needn't show every extreme that they name: `pulse_order`: each row is a permutation of 0 .. 3.
All inputs are finite; a program needn't handle non-finite values.
Results may differ from the reference program's by a relative error of at most 0.0065.
Values may be sent and summed in bfloat16 or wider, within the bound.
No kernel may reach another device: no remote copies, remote signals or barrier semaphores. Data moves between devices by JAX's collectives and lax.ppermute only.
A program may use at most 192 MiB of HBM per device.

```python
import jax
import jax.numpy as jnp
from jax import lax

RAW = 2048
WIN = 1024
UPS = 2048
BAND = 1024
STEPS = 4
PS = 1
C_T = 4096
P_DEV = 4
PULSES = 512
ROWS = 1024
N_TILE = 16
DEVICES = 128


def place_ends(result, rng, low, top_value):
    dims = result.shape
    spot = [jax.random.randint(jax.random.fold_in(rng, axis), (), 0, dims[axis]) for axis in range(len(dims))]
    result = result.at[tuple(spot)].set(low)
    longest = dims.index(max(dims))
    spot[longest] = (spot[longest] + 1) % dims[longest]
    return result.at[tuple(spot)].set(top_value)


def block_scale(key, extent, shards, smallest, top_value):
    gain, own = 1.0, jax.random.fold_in(key, 6)
    for dim, parts in shards:
        draws = jnp.exp(jax.random.uniform(jax.random.fold_in(own, dim), (parts,), jnp.float32, smallest / len(shards), top_value / len(shards)))
        gain = gain * jnp.repeat(draws, extent[dim] // parts).reshape([-1 if axis == dim else 1 for axis in range(len(extent))])
    return gain


def gaussian(stream_key, extent, deviation, most, split=(), held_as=jnp.bfloat16):
    result = deviation * jax.random.normal(stream_key, extent, jnp.float32)
    if split:
        result = result * block_scale(stream_key, extent, split, -0.22, 0.18)
    return jnp.clip(result, -most, most).astype(held_as)


def setup_inputs(seed: int = 0) -> dict:
    seeds = jax.random.split(jax.random.key(seed), 8)
    return {
        "raw": gaussian(seeds[0], (2, PULSES, RAW), 1.0, 6.0, ((1, 128),)),
        "filt": gaussian(seeds[1], (2, WIN, UPS), (2 * WIN) ** -0.5, 0.125),
        "range_off": place_ends(jax.random.randint(seeds[2], (PULSES,), 0, RAW - WIN + 1), jax.random.fold_in(seeds[2], 1), 0, RAW - WIN).astype(jnp.int32),
        "fine": place_ends(jax.random.randint(seeds[3], (PULSES,), 0, 4), jax.random.fold_in(seeds[3], 1), 0, 3).astype(jnp.int32),
        "dop": place_ends(jax.random.randint(seeds[4], (PULSES,), 0, ROWS), jax.random.fold_in(seeds[4], 1), 0, ROWS - 1).astype(jnp.int32),
        "pulse_order": jax.vmap(lambda own: jax.random.permutation(own, P_DEV))(jax.random.split(seeds[5], DEVICES)).reshape((DEVICES, P_DEV)).astype(jnp.int32),
        "band_idx": place_ends(jax.random.randint(seeds[6], (N_TILE, PULSES), 0, UPS - BAND), jax.random.fold_in(seeds[6], 1), 0, (UPS - BAND) - 1).astype(jnp.int32),
    }


def compress(windows, filt):
    wr = windows[:, 0]
    wi = windows[:, 1]
    prof_re = jnp.dot(wr, filt[0], preferred_element_type=jnp.float32) - jnp.dot(wi, filt[1], preferred_element_type=jnp.float32)
    prof_im = jnp.dot(wr, filt[1], preferred_element_type=jnp.float32) + jnp.dot(wi, filt[0], preferred_element_type=jnp.float32)
    return jnp.stack([prof_re, prof_im], 1).astype(jnp.bfloat16)

def cut_band(profile, start):
    segment = lax.dynamic_slice_in_dim(profile, start, BAND + 1, 1)
    return (segment[:, :BAND], segment[:, BAND])

def interpolate(pieces, edges, shifts):
    first = pieces.astype(jnp.float32)
    second = jnp.concatenate([first[..., 1:], edges.astype(jnp.float32)[..., None]], -1)
    first = jnp.repeat(first, 4, axis=-1)
    second = jnp.repeat(second, 4, axis=-1)
    phase_q = (jnp.arange(4 * BAND, dtype=jnp.int32) % 4).astype(jnp.float32)
    weight = (4.0 * phase_q[None, :] + shifts.astype(jnp.float32)[:, None]) / 16.0
    weight = weight[:, None, :]
    return first * (1.0 - weight) + second * weight

def reference(raw, filt, range_off, fine, dop, pulse_order, band_idx):
    devices = pulse_order.shape[0]
    p_dev = pulse_order.shape[1]
    pulses = p_dev * devices
    owners = jnp.arange(devices, dtype=jnp.int32)[:, None] * p_dev
    rows = jnp.arange(ROWS, dtype=jnp.int32)
    lefts = []
    rights = []
    for step in range(STEPS):
        chosen = (owners + pulse_order[:, step * PS:(step + 1) * PS]).reshape(-1).astype(jnp.int32)
        picked = jnp.take(raw, chosen, axis=1)
        offsets = jnp.take(range_off, chosen)
        windows = jax.vmap(lambda row, off: lax.dynamic_slice_in_dim(row, off, WIN, 1), in_axes=(1, 0))(picked, offsets)
        profile = compress(windows, filt)
        starts = jnp.take(band_idx, chosen, axis=1)
        shifts = jnp.take(fine, chosen)
        pieces, edges = jax.vmap(jax.vmap(cut_band, in_axes=(0, 0)), in_axes=(None, 0))(profile, starts)
        samples = jax.vmap(interpolate, in_axes=(0, 0, None))(pieces, edges, shifts)
        summed = lax.optimization_barrier(jnp.sum(samples, axis=1))
        sr = samples[:, :, 0]
        si = samples[:, :, 1]
        rr = summed[:, None, 0]
        ri = summed[:, None, 1]
        g_re = lax.optimization_barrier(jnp.sum(sr * rr + si * ri, axis=(0, 2)))
        g_im = lax.optimization_barrier(jnp.sum(si * rr - sr * ri, axis=(0, 2)))
        scale = jnp.sqrt(g_re * g_re + g_im * g_im + 1.0)
        c_re = (g_re / scale)[None, :, None]
        c_im = (-g_im / scale)[None, :, None]
        new_re = c_re * sr - c_im * si
        new_im = c_re * si + c_im * sr
        rights.append(jnp.concatenate([new_re, new_im], 1).astype(jnp.bfloat16))
        dops = jnp.take(dop, chosen)
        angle = 2.0 * jnp.pi * (dops[:, None] * rows[None, :] % ROWS).astype(jnp.float32) / ROWS
        e_re = (jnp.cos(angle) / jnp.sqrt(jnp.float32(pulses))).astype(jnp.bfloat16)
        e_im = (jnp.sin(angle) / jnp.sqrt(jnp.float32(pulses))).astype(jnp.bfloat16)
        lefts.append(jnp.stack([jnp.concatenate([e_re, -e_im], 0), jnp.concatenate([e_im, e_re], 0)], 0))
    left_all = jnp.concatenate(lefts, 1).astype(jnp.float32)
    right_all = jnp.concatenate(rights, 1)

    def one_tile(right):
        return jnp.einsum('zkr,kc->zrc', left_all, right.astype(jnp.float32)).astype(jnp.bfloat16)
    tiles = lax.map(one_tile, right_all)
    n_tile = tiles.shape[0]
    return jnp.transpose(tiles, (1, 2, 0, 3)).reshape(2, ROWS, n_tile * C_T)
```

```python
import jax
import jax.numpy as jnp
from jax import lax
from jax.experimental import pallas as pl
from jax.experimental.pallas import tpu as pltpu
from jax.sharding import PartitionSpec as P

AXES = ("pulse", "tile")
WIN = 1024
UPS = 2048
MSG = 2 * WIN + 128
GROUP = 64
HALF = 256
BW = 1152
ROWS = 128
STEPS = (0, 1, 3, 2)
F32 = jnp.float32
BF16 = jnp.bfloat16
NT = (((1,), (1,)), ((), ()))


def linear(z, y, x, core):
    return (z * 2 + y % 2) * 16 + ((y // 2) * 4 + x) * 2 + core


def moves(target):
    return [
        (linear(z, y, x, c), linear(*target(z, y, x, c)))
        for z in range(4)
        for y in range(4)
        for x in range(4)
        for c in range(2)
    ]


def along_z(k):
    return moves(lambda z, y, x, c: ((z + k) % 4, y, x, c))


def along_y(k):
    return moves(lambda z, y, x, c: (z, (y + k) % 4, x, c))


def along_x(k):
    return moves(lambda z, y, x, c: (z, y, (x + k) % 4, c))


def other_core():
    return moves(lambda z, y, x, c: (z, y, x, 1 - c))


def iota(shape, axis):
    return lax.broadcasted_iota(jnp.int32, shape, axis)


def window_kernel(order, off, fine, dop, band, raw, out):
    x = jnp.concatenate([raw[0].astype(F32), raw[1].astype(F32)], 0)
    row8 = iota((8, WIN), 0)
    row4 = iota((4, WIN), 0)
    lane = iota((1, 128), 1)
    meta_row = iota((4, 128), 0)
    re = jnp.zeros((4, WIN), F32)
    im = jnp.zeros((4, WIN), F32)
    meta = jnp.zeros((4, 128), jnp.int32)
    for j in range(4):
        k = order[0, j]
        y = pltpu.roll(x, lax.rem(UPS - off[k], UPS), 1)[:, :WIN]
        one_re = jnp.sum(jnp.where(row8 == k, y, 0.0), axis=0, keepdims=True)
        one_im = jnp.sum(jnp.where(row8 == k + 4, y, 0.0), axis=0, keepdims=True)
        re = jnp.where(row4 == j, one_re, re)
        im = jnp.where(row4 == j, one_im, im)
        d = dop[k]
        v = jnp.where(lane == 1, fine[k], 0)
        v = jnp.where(lane == 2, d >> 5, v)
        v = jnp.where(lane == 3, d & 31, v)
        for t in range(16):
            b = band[t, k]
            v = jnp.where(lane == 16 + t, b >> 5, v)
            v = jnp.where(lane == 32 + t, b & 31, v)
        meta = jnp.where(meta_row == j, v, meta)
    out[:, :WIN] = re.astype(BF16)
    out[:, WIN : 2 * WIN] = im.astype(BF16)
    out[:, 2 * WIN :] = meta.astype(F32).astype(BF16)


def band_kernel(m0, m1, m2, m3, filt, mine, theirs, w, info, prof, cut, starts_v, starts_s, sem):
    n = pl.program_id(0)
    tile = lax.axis_index("tile")

    @pl.when(n == 0)
    def _():
        x_here = lax.rem(tile // 2, 4)
        y_here = tile // 8 * 2 + lax.rem(lax.axis_index("pulse"), 2)
        for m, dx in zip((m0, m1, m2, m3), STEPS):
            from_x = lax.rem(x_here + 4 - dx, 4)
            for i, dy in enumerate(STEPS):
                from_y = lax.rem(y_here + 4 - dy, 4)
                at = pl.multiple_of(from_x * GROUP + from_y * 16, 16)
                wr = m[16 * i : 16 * i + 16, :WIN]
                wi = m[16 * i : 16 * i + 16, WIN : 2 * WIN]
                w[pl.ds(at, 16), :WIN] = wr
                w[pl.ds(at, 16), WIN:] = -wi
                w[pl.ds(at + HALF, 16), :WIN] = wi
                w[pl.ds(at + HALF, 16), WIN:] = wr
                info[pl.ds(at, 16), :] = m[16 * i : 16 * i + 16, 2 * WIN :]

    f = filt[...].reshape(2 * WIN, 256)
    r = jnp.dot(w[...], f, preferred_element_type=F32)
    for comp in range(2):
        for h in range(2):
            base = pl.multiple_of((comp * 16 + 2 * n + h) * 8, 8)
            for g in range(32):
                prof[pl.ds(base + g * 256, 8), :] = r[
                    comp * HALF + 8 * g : comp * HALF + 8 * g + 8, 128 * h : 128 * h + 128
                ]

    @pl.when(n == 7)
    def _():
        sibling = tile + 1 - 2 * lax.rem(tile, 2)
        row = iota((8, 128), 0)
        lane = iota((8, 128), 1)
        want = jnp.where(row == 0, tile, sibling)
        pick = jnp.where(lane == want + 16, 32.0, jnp.where(lane == want + 32, 1.0, 0.0)).astype(BF16)
        got = lax.dot_general(pick, info[...], NT, preferred_element_type=F32)
        starts_v[...] = got.astype(jnp.int32)
        copy = pltpu.make_async_copy(starts_v, starts_s, sem)
        copy.start()
        copy.wait()
        lane8 = iota((8, 128), 1)

        def per_group(g, _):
            for sub in range(8):
                for which in range(2):
                    start = starts_s[which, g * 8 + sub]
                    a = start >> 7
                    r = start & 127
                    turn = (128 - r) & 127
                    inside = lane8 < 128 - r
                    for comp in range(2):
                        at = g * 256 + (comp * 16 + a) * 8 + sub
                        low = pltpu.roll(prof[pl.ds(at, 8, 8), :], turn, 1)
                        high = pltpu.roll(prof[pl.ds(at + 8, 8, 8), :], turn, 1)
                        to = g * 144 + comp * 72 + sub
                        cut[which, pl.ds(to + 8, 8, 8), :] = high
                        cut[which, pl.ds(to, 8, 8), :] = jnp.where(inside, low, high)
            return 0

        lax.fori_loop(0, 32, per_group, 0)
        lane16 = iota((16, 128), 1)
        for which, out in enumerate((mine, theirs)):
            for top in range(0, HALF, 16):
                meta = info[top : top + 16, :].astype(F32)
                for comp in range(2):
                    for c in range(9):
                        at = (top // 8) * 144 + comp * 72 + c * 8
                        v = jnp.concatenate(
                            [cut[which, at : at + 8, :], cut[which, at + 144 : at + 152, :]], 0
                        )
                        if c == 8:
                            v = jnp.where(lane16 == 0, v, jnp.where(lane16 < 4, meta, 0.0))
                        to = comp * HALF + top
                        out[to : to + 16, 128 * c : 128 * c + 128] = v.astype(BF16)


def gradient_kernel(ba, bb, g_out, meta_out):
    row = iota((8, 128), 0)
    lane = iota((8, 128), 1)
    pick = jnp.where(
        row == 0,
        jnp.where(lane == 1, 1.0, 0.0),
        jnp.where(lane == 2, 32.0, jnp.where(lane == 3, 1.0, 0.0)),
    ).astype(BF16)
    block = iota((8, HALF), 0) % 4
    keep = jnp.where(iota((8, HALF), 1) % 4 == block, 1.0, 0.0)
    sums_re = jnp.zeros((16, BW), F32)
    sums_im = jnp.zeros((16, BW), F32)
    weights = []
    for i, b in enumerate((ba, bb)):
        meta = lax.dot_general(pick, b[:HALF, WIN:], NT, preferred_element_type=F32)
        meta_out[:, HALF * i : HALF * (i + 1)] = meta
        shift = meta[0:1] / 16.0
        lhs = jnp.concatenate([keep, keep * shift], 0).astype(BF16)
        sums_re += jnp.dot(lhs, b[:HALF], preferred_element_type=F32)
        sums_im += jnp.dot(lhs, b[HALF:], preferred_element_type=F32)
        weights.append(jnp.where(iota((8, HALF), 0) < 4, keep, keep * shift))
    m = iota((8, BW), 1)
    top = iota((8, BW), 0) < 4
    parts = []
    for sums in (sums_re, sums_im):
        s = sums[:8]
        t = sums[8:]
        x0 = s + pltpu.roll(t, BW - 1, 1) - t
        dr = pltpu.roll(s, BW - 1, 1) - s
        a = jnp.where(m < WIN, 4.0 * x0 + 1.5 * dr, 0.0)
        b = jnp.where(m < WIN, 1.5 * x0 + 0.875 * dr, 0.0)
        p = a - b + pltpu.roll(b, 1, 1)
        q = pltpu.roll(a, 1, 1) - a
        parts.append(jnp.where(top, p, q))
    both = jnp.concatenate(parts, 0)
    high = both.astype(BF16)
    low = (both - high.astype(F32)).astype(BF16)
    lhs = jnp.concatenate([high, low], 0)
    halves = []
    for i, b in enumerate((ba, bb)):
        g = lax.dot_general(lhs, b[...], NT, preferred_element_type=F32)
        g = g[:16] + g[16:]
        re = g[:8, :HALF] + g[8:, HALF:]
        im = g[:8, HALF:] - g[8:, :HALF]
        g_re = jnp.sum(re * weights[i], axis=0, keepdims=True)
        g_im = jnp.sum(im * weights[i], axis=0, keepdims=True)
        halves.append(jnp.concatenate([g_re, g_im], 0))
    first = lax.rem(lax.axis_index("tile"), 2) == 0
    g_out[:, :HALF] = jnp.where(first, halves[0], halves[1])
    g_out[:, HALF:] = jnp.where(first, halves[1], halves[0])


def image_kernel(g, meta, ba, bb, out, lhs, xd):
    first = lax.rem(lax.axis_index("tile"), 2) == 0
    both = jnp.concatenate(
        [jnp.where(first, g[:, :HALF], g[:, HALF:]), jnp.where(first, g[:, HALF:], g[:, :HALF])], 1
    )
    g_re = both[0:1]
    g_im = both[1:2]
    inv = 1.0 / jnp.sqrt(g_re * g_re + g_im * g_im + 1.0)
    inv = inv * (512.0**-0.5)
    c_re = g_re * inv
    c_im = -g_im * inv
    shift = meta[0:1] / 16.0
    dop = meta[1:2].astype(jnp.int32)
    pulse = lax.axis_index("pulse")
    step = 2.0 * jnp.pi / 1024.0
    coarse = ((iota((16, 512), 0) * 8 + pulse * ROWS) * dop & 1023).astype(F32) * step
    finer = (iota((8, 512), 0) * dop & 1023).astype(F32) * step
    cu = jnp.cos(coarse)
    su = jnp.sin(coarse)
    cv = jnp.cos(finer)
    sv = jnp.sin(finer)
    vr = cv * c_re - sv * c_im
    vi = cv * c_im + sv * c_re
    for u in range(16):
        ur = cu[u : u + 1]
        ui = su[u : u + 1]
        lr = ur * vr - ui * vi
        li = ur * vi + ui * vr
        for scale, at in ((None, 0), (shift, 256)):
            r = lr if scale is None else lr * scale
            i = li if scale is None else li * scale
            for half in range(2):
                rr = r[:, HALF * half : HALF * (half + 1)]
                ii = i[:, HALF * half : HALF * (half + 1)]
                a = at + 8 * u
                lhs[a : a + 8, 512 * half : 512 * half + HALF] = rr
                lhs[a : a + 8, 512 * half + HALF : 512 * half + 512] = -ii
                lhs[a + 128 : a + 136, 512 * half : 512 * half + HALF] = ii
                lhs[a + 128 : a + 136, 512 * half + HALF : 512 * half + 512] = rr
    uv = jnp.dot(lhs[:, :512].astype(BF16), ba[...], preferred_element_type=F32) + jnp.dot(
        lhs[:, 512:].astype(BF16), bb[...], preferred_element_type=F32
    )
    later = pltpu.roll(uv, BW - 1, 1)
    diff = later - uv
    xd[:, :WIN] = (uv[:256] + diff[256:])[:, :WIN].astype(BF16)
    xd[:, WIN:] = diff[:256, :WIN].astype(BF16)
    k = iota((256, 512), 0)
    col = iota((256, 512), 1)
    same = (k % 128) == (col // 4)
    quarter = (col % 4).astype(F32) * 0.25
    spread = jnp.where(same, jnp.where(k < 128, 1.0, quarter), 0.0).astype(BF16)
    for j in range(8):
        part = jnp.concatenate(
            [xd[:, 128 * j : 128 * j + 128], xd[:, WIN + 128 * j : WIN + 128 * j + 128]], 1
        )
        res = jnp.dot(part, spread, preferred_element_type=F32).astype(BF16)
        out[0, :, 512 * j : 512 * j + 512] = res[:128]
        out[1, :, 512 * j : 512 * j + 512] = res[128:]


def vmem():
    return pl.BlockSpec(memory_space=pltpu.VMEM)


def smem():
    return pl.BlockSpec(memory_space=pltpu.SMEM)


def params():
    return pltpu.CompilerParams(vmem_limit_bytes=48 * 1024 * 1024)


def shards(raw, filt, range_off, fine, dop, pulse_order, band_idx):
    own = pl.pallas_call(
        window_kernel,
        out_shape=jax.ShapeDtypeStruct((4, MSG), BF16),
        in_specs=[smem()] * 5 + [vmem()],
        out_specs=vmem(),
        compiler_params=params(),
    )(pulse_order, range_off, fine, dop, band_idx, raw)
    line = jnp.concatenate([own] + [lax.ppermute(own, AXES, along_z(k)) for k in STEPS[1:]], 0)
    plane = jnp.concatenate([line] + [lax.ppermute(line, AXES, along_y(k)) for k in STEPS[1:]], 0)
    groups = [plane] + [lax.ppermute(plane, AXES, along_x(k)) for k in STEPS[1:]]
    whole = pl.BlockSpec((GROUP, MSG), lambda n: (0, 0))
    mine, theirs = pl.pallas_call(
        band_kernel,
        grid=(8,),
        out_shape=[jax.ShapeDtypeStruct((2 * HALF, BW), BF16)] * 2,
        in_specs=[whole] * 4 + [pl.BlockSpec((2, WIN, 256), lambda n: (0, 0, n))],
        out_specs=[pl.BlockSpec((2 * HALF, BW), lambda n: (0, 0))] * 2,
        scratch_shapes=[
            pltpu.VMEM((2 * HALF, 2 * WIN), BF16),
            pltpu.VMEM((HALF, 128), BF16),
            pltpu.VMEM((8192, 128), F32),
            pltpu.VMEM((2, 4608, 128), F32),
            pltpu.VMEM((8, HALF), jnp.int32),
            pltpu.SMEM((8, HALF), jnp.int32),
            pltpu.SemaphoreType.DMA,
        ],
        compiler_params=params(),
    )(*groups, filt)
    given = lax.ppermute(theirs, AXES, other_core())
    partial, meta = pl.pallas_call(
        gradient_kernel,
        out_shape=[jax.ShapeDtypeStruct((2, 512), F32), jax.ShapeDtypeStruct((8, 512), F32)],
        in_specs=[vmem()] * 2,
        out_specs=[vmem()] * 2,
        compiler_params=params(),
    )(mine, given)
    sent = jnp.broadcast_to(partial[None], (16, 2, 512))
    grads = jnp.sum(lax.all_to_all(sent, "tile", split_axis=0, concat_axis=0, tiled=True), axis=0)
    return pl.pallas_call(
        image_kernel,
        out_shape=jax.ShapeDtypeStruct((2, ROWS, 4 * WIN), BF16),
        in_specs=[vmem()] * 4,
        out_specs=vmem(),
        scratch_shapes=[pltpu.VMEM((512, 1024), F32), pltpu.VMEM((256, 2 * WIN), BF16)],
        compiler_params=params(),
    )(grads, meta, mine, given)


def solution(mesh):
    return jax.shard_map(
        shards,
        mesh=mesh,
        in_specs=(
            P(None, AXES, None),
            P(),
            P(AXES),
            P(AXES),
            P(AXES),
            P(AXES, None),
            P(None, AXES),
        ),
        out_specs=P(None, "pulse", "tile"),
        check_vma=False,
    )
```

```python
import jax
import jax.numpy as jnp
from jax import lax
from jax.experimental import pallas as pl
from jax.experimental.pallas import tpu as pltpu
from jax.sharding import PartitionSpec as P

AXES = ("pulse", "tile")
WIN = 1024
UPS = 2048
BW = WIN + 128
ROWS = 128
CHUNK = 128
STEPS = (0, 1, 3, 2)
F32 = jnp.float32
BF16 = jnp.bfloat16
NT = (((1,), (1,)), ((), ()))
MIB = 1024 * 1024


def linear(z, y, x, core):
    return (z * 2 + y % 2) * 16 + ((y // 2) * 4 + x) * 2 + core


PLACES = [(z, y, x, c) for z in range(4) for y in range(4) for x in range(4) for c in range(2)]


def planes():
    groups = {}
    for z, y, x, c in PLACES:
        groups.setdefault((c, x if c == 0 else y), []).append(linear(z, y, x, c))
    return [groups[key] for key in sorted(groups)]


def along_last(k):
    return [
        (
            linear(z, y, x, c),
            linear(z, y, (x + k) % 4, c) if c == 0 else linear(z, (y + k) % 4, x, c),
        )
        for z, y, x, c in PLACES
    ]


def other_core():
    return [(linear(z, y, x, c), linear(z, y, x, 1 - c)) for z, y, x, c in PLACES]


def iota(shape, axis):
    return lax.broadcasted_iota(jnp.int32, shape, axis)


def window_kernel(order_h, off_h, fine_h, dop_h, band_h, raw_h, out, order, off, fine, dop, band, raw, sems):
    pairs = ((order_h, order), (off_h, off), (fine_h, fine), (dop_h, dop), (band_h, band), (raw_h, raw))
    copies = [pltpu.make_async_copy(a, b, sems.at[i]) for i, (a, b) in enumerate(pairs)]
    for copy in copies:
        copy.start()
    for copy in copies:
        copy.wait()
    x = jnp.concatenate([raw[0].astype(F32), raw[1].astype(F32)], 0)
    row = iota((8, WIN), 0)
    lane = iota((1, 128), 1)
    meta_row = iota((8, 128), 0)
    both = jnp.zeros((8, WIN), F32)
    meta = jnp.zeros((8, 128), jnp.int32)
    for j in range(4):
        k = order[0, j]
        y = pltpu.roll(x, lax.rem(UPS - off[k], UPS), 1)[:, :WIN]
        one_re = jnp.sum(jnp.where(row == k, y, 0.0), axis=0, keepdims=True)
        one_im = jnp.sum(jnp.where(row == k + 4, y, 0.0), axis=0, keepdims=True)
        both = jnp.where(row == j, one_re, jnp.where(row == j + 4, one_im, both))
        d = dop[k]
        v = jnp.where(lane == 1, fine[k], 0)
        v = jnp.where(lane == 2, d >> 5, v)
        v = jnp.where(lane == 3, d & 31, v)
        for t in range(16):
            b = band[k, t]
            v = jnp.where(lane == 16 + t, b >> 5, v)
            v = jnp.where(lane == 32 + t, b & 31, v)
        meta = jnp.where((meta_row & 3) == j, v, meta)
    both = both.astype(BF16)
    meta = meta.astype(F32).astype(BF16)
    for i in range(16):
        out[i, :, :WIN] = both
        out[i, :, WIN:] = meta


def band_kernel(m, filt, theirs, mine, w, prof, cut, starts_v, starts_s, sem):
    tile = lax.axis_index("tile")
    sibling = tile + 1 - 2 * lax.rem(tile, 2)
    lane8 = iota((8, 128), 1)
    row8 = iota((8, 128), 0)
    info = m[:, WIN:]
    want = jnp.where(row8 == 0, tile, sibling)
    pick = jnp.where(lane8 == want + 16, 32.0, jnp.where(lane8 == want + 32, 1.0, 0.0)).astype(BF16)
    starts_v[...] = lax.dot_general(pick, info, NT, preferred_element_type=F32).astype(jnp.int32)
    copy = pltpu.make_async_copy(starts_v, starts_s, sem)
    copy.start()
    k = iota((128, 256), 0)
    want = jnp.where(iota((128, 256), 1) < 128, tile, sibling)
    spread = jnp.where(k == want + 16, 32.0, jnp.where(k == want + 32, 1.0, 0.0)).astype(BF16)
    turns = jnp.dot(info, spread, preferred_element_type=F32).astype(jnp.int32) & 127

    sign = jnp.where(iota((8, WIN), 0) < 4, -1.0, 1.0)
    w[:, :WIN] = m[:, :WIN]
    for g in range(0, CHUNK, 16):
        v = m[g : g + 16, :WIN].astype(F32)
        top = pltpu.roll(v[:8], 4, 0) * sign
        low = pltpu.roll(v[8:], 4, 0) * sign
        w[g : g + 16, WIN:] = jnp.concatenate([top, low], 0).astype(BF16)
    for n in range(0, UPS, 512):
        f = filt[:, :, n : n + 512].reshape(2 * WIN, 512)
        r = jnp.dot(w[...], f, preferred_element_type=F32)
        for h in range(4):
            for g in range(16):
                at = g * 128 + (n // 128 + h) * 8
                prof[at : at + 8, :] = r[8 * g : 8 * g + 8, 128 * h : 128 * h + 128]
    copy.wait()
    for which, out in enumerate((theirs, mine)):
        for g in range(16):
            for j in range(4):
                start = starts_s[1 - which, 8 * g + j]
                turn = (128 - (start & 127)) & 127
                at = g * 128 + (start >> 7) * 8 + j
                re = pltpu.roll(prof[pl.ds(at, 8, 8), :], turn, 1)
                im = pltpu.roll(prof[pl.ds(at + 4, 8, 8), :], turn, 1)
                end = pltpu.roll(prof[pl.ds(at + 64, 2, 4), :], turn, 1)
                to = g * 72 + j
                cut[which, pl.ds(to, 8, 8), :] = re
                cut[which, pl.ds(to + 4, 8, 8), :] = im
                cut[which, pl.ds(to + 64, 2, 4), :] = end
    for which, out in enumerate((theirs, mine)):
        for pair in range(8):
            done = [[], []]
            for e in range(2):
                g = 2 * pair + e
                turn = turns[8 * g : 8 * g + 8, 128 * (1 - which) : 128 * (1 - which) + 128]
                inside = lane8 + turn < 128
                parts = [cut[which, g * 72 + 8 * c : g * 72 + 8 * c + 8, :] for c in range(9)]
                done[e] = [jnp.where(inside, parts[c], parts[c + 1]) for c in range(8)]
                meta = info[8 * g : 8 * g + 8].astype(F32)
                done[e].append(
                    jnp.where(lane8 == 0, parts[8], jnp.where(lane8 < 4, meta, 0.0))
                )
            for c in range(9):
                v = jnp.concatenate([done[0][c], done[1][c]], 0).astype(BF16)
                out[16 * pair : 16 * pair + 16, 128 * c : 128 * c + 128] = v


def positions():
    tile = lax.axis_index("tile")
    core = lax.rem(tile, 2)
    x = lax.rem(tile // 2, 4)
    y = tile // 8 * 2 + lax.rem(lax.axis_index("pulse"), 2)
    own = jnp.where(core == 0, x, y)
    other = jnp.where(core == 0, y, x)
    return [core * 4 + lax.rem(own + 4 - k, 4) for k in STEPS] + [
        (1 - core) * 4 + lax.rem(other + 4 - k, 4) for k in STEPS
    ]


def gradient_kernel(*refs):
    parts = refs[:8]
    g_out, meta_out, b = refs[8:11]
    place = refs[11]
    for i, part in enumerate(parts):
        b[CHUNK * i : CHUNK * (i + 1), :] = part[...]
    row8 = iota((8, 128), 0)
    lane8 = iota((8, 128), 1)
    pick = jnp.where(
        row8 == 0,
        jnp.where(lane8 == 1, 1.0, 0.0),
        jnp.where(row8 == 1, jnp.where(lane8 == 2, 32.0, jnp.where(lane8 == 3, 1.0, 0.0)), 0.0),
    ).astype(BF16)
    meta = lax.dot_general(pick, b[:, WIN:], NT, preferred_element_type=F32)
    for i in range(8):
        meta_out[0, i : i + 1, :] = meta[0:1, CHUNK * i : CHUNK * (i + 1)]
        meta_out[1, i : i + 1, :] = meta[1:2, CHUNK * i : CHUNK * (i + 1)]
    shift = meta[0:1] * 0.0625
    keep = jnp.where((iota((8, WIN), 1) & 7) == iota((8, WIN), 0), 1.0, 0.0)
    lhs = jnp.concatenate([keep, keep * shift], 0).astype(BF16)
    sums = jnp.dot(lhs, b[...], preferred_element_type=F32)
    s = sums[:8]
    t = sums[8:]
    inner = iota((8, BW), 1) < WIN
    x0 = s + pltpu.roll(t, BW - 1, 1) - t
    dr = pltpu.roll(s, BW - 1, 1) - s
    a = jnp.where(inner, 4.0 * x0 + 1.5 * dr, 0.0)
    d = jnp.where(inner, 1.5 * x0 + 0.875 * dr, 0.0)
    p = a - d + pltpu.roll(d, 1, 1)
    q = pltpu.roll(a, 1, 1) - a
    both = jnp.concatenate([p, q], 0)
    high = both.astype(BF16)
    low = (both - high.astype(F32)).astype(BF16)
    g = lax.dot_general(jnp.concatenate([high, low], 0), b[...], NT, preferred_element_type=F32)
    g = g[:16] + g[16:]
    g = g[:8] + g[8:] * shift
    j = iota((8, WIN), 1) & 3
    row = iota((8, WIN), 0)
    by_re = jnp.sum(jnp.where(row == j, g, 0.0), axis=0, keepdims=True)
    by_im = jnp.sum(jnp.where(row == j + 4, g, 0.0), axis=0, keepdims=True)
    even = (iota((1, WIN), 1) & 4) == 0
    swapped = jnp.where(even, pltpu.roll(by_im, WIN - 4, 1), -pltpu.roll(by_im, 4, 1))
    grads = by_re + swapped
    for i, at in enumerate(positions()):
        place[pl.ds(at, 1), :] = grads[:, CHUNK * i : CHUNK * (i + 1)]
    for t in range(16):
        g_out[t] = place[...]


def image_kernel(g_in, meta, b, out_h, total, lhs, xd, out, sems):
    total[...] = jnp.sum(g_in[...], axis=0)
    even8 = (iota((8, 128), 1) & 4) == 0
    local = jnp.concatenate([total[pl.ds(at, 1), :] for at in positions()], 0)
    g_re = jnp.where(even8, local, pltpu.roll(local, 4, 1))
    g_im = jnp.where(even8, pltpu.roll(local, 124, 1), local)
    inv = (512.0**-0.5) / jnp.sqrt(g_re * g_re + g_im * g_im + 1.0)
    c_re = jnp.where(even8, g_re, g_im) * inv
    c_im = jnp.where(even8, -g_im, g_re) * inv

    def wide(v):
        return jnp.concatenate([v[i : i + 1] for i in range(8)], 1)

    shift = wide(meta[0]) * 0.0625
    dop = wide(meta[1].astype(jnp.int32))
    c_re = wide(c_re)
    c_im = wide(c_im)
    pulse = lax.axis_index("pulse")
    step = 2.0 * jnp.pi / 1024.0
    coarse = (((iota((16, WIN), 0) * 8 + pulse * ROWS) * dop) & 1023).astype(F32) * step
    finer = ((iota((8, WIN), 0) * dop) & 1023).astype(F32) * step
    cu = jnp.cos(coarse)
    su = jnp.sin(coarse)
    cv = jnp.cos(finer)
    sv = jnp.sin(finer)
    vr = cv * c_re - sv * c_im
    vi = cv * c_im + sv * c_re
    for u in range(0, 16, 2):
        pair = []
        for e in range(2):
            ur = cu[u + e : u + e + 1]
            ui = su[u + e : u + e + 1]
            pair.append((ur * vr - ui * vi, ur * vi + ui * vr))
        at = 8 * u
        for z in range(2):
            v = jnp.concatenate([pair[0][z], pair[1][z]], 0)
            lhs[at + 128 * z : at + 128 * z + 16, :] = v.astype(BF16)
            lhs[at + 256 + 128 * z : at + 272 + 128 * z, :] = (v * shift).astype(BF16)
    uv = jnp.dot(lhs[...], b[...], preferred_element_type=F32)
    diff = pltpu.roll(uv, BW - 1, 1) - uv
    xd[:, :WIN] = (uv[:256] + diff[256:])[:, :WIN].astype(BF16)
    xd[:, WIN:] = diff[:256, :WIN].astype(BF16)
    k = iota((256, 512), 0)
    col = iota((256, 512), 1)
    quarter = (col & 3).astype(F32) * 0.25
    spread = jnp.where((k & 127) == (col >> 2), jnp.where(k < 128, 1.0, quarter), 0.0).astype(BF16)
    copies = []
    for j in range(8):
        at = 128 * j
        part = jnp.concatenate([xd[:, at : at + 128], xd[:, WIN + at : WIN + at + 128]], 1)
        res = jnp.dot(part, spread, preferred_element_type=F32).astype(BF16)
        out[0, :, 512 * j : 512 * j + 512] = res[:128]
        out[1, :, 512 * j : 512 * j + 512] = res[128:]
        block = (slice(None), slice(None), pl.ds(512 * j, 512))
        copies.append(pltpu.make_async_copy(out.at[block], out_h.at[block], sems.at[j]))
        copies[-1].start()
    for copy in copies:
        copy.wait()


def vmem():
    return pl.BlockSpec(memory_space=pltpu.VMEM)


def hbm():
    return pl.BlockSpec(memory_space=pltpu.HBM)


def params(mib):
    return pltpu.CompilerParams(vmem_limit_bytes=mib * MIB)


def cost(flops, size):
    return pl.CostEstimate(flops=flops, bytes_accessed=size, transcendentals=0)


def shards(raw, filt, range_off, fine, dop, pulse_order, band_idx):
    own = pl.pallas_call(
        window_kernel,
        out_shape=jax.ShapeDtypeStruct((16, 8, BW), BF16),
        in_specs=[hbm()] * 6,
        out_specs=vmem(),
        scratch_shapes=[
            pltpu.SMEM((1, 4), jnp.int32),
            pltpu.SMEM((4,), jnp.int32),
            pltpu.SMEM((4,), jnp.int32),
            pltpu.SMEM((4,), jnp.int32),
            pltpu.SMEM((4, 16), jnp.int32),
            pltpu.VMEM((2, 4, UPS), BF16),
            pltpu.SemaphoreType.DMA((6,)),
        ],
        compiler_params=params(8),
    )(pulse_order, range_off, fine, dop, band_idx.T, raw)
    plane = lax.all_to_all(
        own, AXES, split_axis=0, concat_axis=0, axis_index_groups=planes(), tiled=True
    ).reshape(CHUNK, BW)
    chunks = [plane] + [lax.ppermute(plane, AXES, along_last(k)) for k in STEPS[1:]]
    bands = pl.pallas_call(
        band_kernel,
        out_shape=[jax.ShapeDtypeStruct((CHUNK, BW), BF16)] * 2,
        in_specs=[vmem()] * 2,
        out_specs=[vmem()] * 2,
        scratch_shapes=[
            pltpu.VMEM((CHUNK, 2 * WIN), BF16),
            pltpu.VMEM((2048, 128), F32),
            pltpu.VMEM((2, 16 * 72, 128), F32),
            pltpu.VMEM((8, 128), jnp.int32),
            pltpu.SMEM((8, 128), jnp.int32),
            pltpu.SemaphoreType.DMA,
        ],
        compiler_params=params(12),
        cost_estimate=cost(2 * CHUNK * UPS * UPS, 8 * MIB),
    )
    mine = []
    given = []
    for chunk in chunks:
        theirs, ours = bands(chunk, filt)
        mine.append(ours)
        given.append(lax.ppermute(theirs, AXES, other_core()))
    partial, meta, b = pl.pallas_call(
        gradient_kernel,
        out_shape=[
            jax.ShapeDtypeStruct((16, 8, 128), F32),
            jax.ShapeDtypeStruct((2, 8, 128), F32),
            jax.ShapeDtypeStruct((WIN, BW), BF16),
        ],
        in_specs=[vmem()] * 8,
        out_specs=[vmem()] * 3,
        scratch_shapes=[pltpu.VMEM((8, 128), F32)],
        compiler_params=params(12),
    )(*mine, *given)
    grads = lax.all_to_all(partial, "tile", split_axis=0, concat_axis=0, tiled=True)
    return pl.pallas_call(
        image_kernel,
        out_shape=jax.ShapeDtypeStruct((2, ROWS, 4 * WIN), BF16),
        in_specs=[vmem()] * 3,
        out_specs=hbm(),
        scratch_shapes=[
            pltpu.VMEM((8, 128), F32),
            pltpu.VMEM((512, WIN), BF16),
            pltpu.VMEM((256, 2 * WIN), BF16),
            pltpu.VMEM((2, ROWS, 4 * WIN), BF16),
            pltpu.SemaphoreType.DMA((8,)),
        ],
        compiler_params=params(20),
    )(grads, meta, b)


def solution(mesh):
    return jax.shard_map(
        shards,
        mesh=mesh,
        in_specs=(
            P(None, AXES, None),
            P(),
            P(AXES),
            P(AXES),
            P(AXES),
            P(AXES, None),
            P(None, AXES),
        ),
        out_specs=P(None, "pulse", "tile"),
        check_vma=False,
    )
```

```python
import jax
import jax.numpy as jnp
from jax import lax
from jax.experimental import pallas as pl
from jax.experimental.pallas import tpu as pltpu
from jax.sharding import PartitionSpec as P

AXES = ("pulse", "tile")
WIN = 1024
UPS = 2048
BW = WIN + 128
ROWS = 128
CHUNK = 128
STEPS = (0, 1, 3, 2)
F32 = jnp.float32
BF16 = jnp.bfloat16
NT = (((1,), (1,)), ((), ()))
MIB = 1024 * 1024
FIRST = 42


def linear(z, y, x, core):
    return (z * 2 + y % 2) * 16 + ((y // 2) * 4 + x) * 2 + core


PLACES = [(z, y, x, c) for z in range(4) for y in range(4) for x in range(4) for c in range(2)]


def planes():
    groups = {}
    for z, y, x, c in PLACES:
        groups.setdefault((c, x if c == 0 else y), []).append(linear(z, y, x, c))
    return [groups[key] for key in sorted(groups)]


def along_last(k):
    return [
        (
            linear(z, y, x, c),
            linear(z, y, (x + k) % 4, c) if c == 0 else linear(z, (y + k) % 4, x, c),
        )
        for z, y, x, c in PLACES
    ]


def other_core():
    return [(linear(z, y, x, c), linear(z, y, x, 1 - c)) for z, y, x, c in PLACES]


def iota(shape, axis):
    return lax.broadcasted_iota(jnp.int32, shape, axis)


def window_kernel(order_h, off_h, fine_h, dop_h, band_h, raw_h, out, order, off, fine, dop, band, raw, sems):
    pairs = ((order_h, order), (off_h, off), (fine_h, fine), (dop_h, dop), (band_h, band), (raw_h, raw))
    copies = [pltpu.make_async_copy(a, b, sems.at[i]) for i, (a, b) in enumerate(pairs)]
    for copy in copies:
        copy.start()
    for copy in copies:
        copy.wait()
    x = jnp.concatenate([raw[0].astype(F32), raw[1].astype(F32)], 0)
    row = iota((8, WIN), 0)
    lane = iota((1, 128), 1)
    meta_row = iota((8, 128), 0)
    both = jnp.zeros((8, WIN), F32)
    meta = jnp.zeros((8, 128), jnp.int32)
    for j in range(4):
        k = order[0, j]
        y = pltpu.roll(x, lax.rem(UPS - off[k], UPS), 1)[:, :WIN]
        one_re = jnp.sum(jnp.where(row == k, y, 0.0), axis=0, keepdims=True)
        one_im = jnp.sum(jnp.where(row == k + 4, y, 0.0), axis=0, keepdims=True)
        both = jnp.where(row == j, one_re, jnp.where(row == j + 4, one_im, both))
        d = dop[k]
        v = jnp.where(lane == 1, fine[k], 0)
        v = jnp.where(lane == 2, d >> 5, v)
        v = jnp.where(lane == 3, d & 31, v)
        for t in range(16):
            b = band[k, t]
            v = jnp.where(lane == 16 + t, b >> 5, v)
            v = jnp.where(lane == 32 + t, b & 31, v)
        meta = jnp.where((meta_row & 3) == j, v, meta)
    both = both.astype(BF16)
    meta = meta.astype(F32).astype(BF16)
    for i in range(16):
        out[i, :, :WIN] = both
        out[i, :, WIN:] = meta


def first_band_kernel(m, filt_h, theirs, mine, filt, w, prof, cut, starts_v, starts_s, sem, sems):
    copies = []
    for i in range(4):
        block = (slice(None), slice(None), pl.ds(512 * i, 512))
        copies.append(pltpu.make_async_copy(filt_h.at[block], filt.at[block], sems.at[i]))
        copies[-1].start()
    band_kernel(m, filt, theirs, mine, w, prof, cut, starts_v, starts_s, sem, copies)


def band_kernel(m, filt, theirs, mine, w, prof, cut, starts_v, starts_s, sem, copies=None):
    tile = lax.axis_index("tile")
    sibling = tile + 1 - 2 * lax.rem(tile, 2)
    lane8 = iota((8, 128), 1)
    row8 = iota((8, 128), 0)
    info = m[:, WIN:]
    want = jnp.where(row8 == 0, tile, sibling)
    pick = jnp.where(lane8 == want + 16, 32.0, jnp.where(lane8 == want + 32, 1.0, 0.0)).astype(BF16)
    starts_v[...] = lax.dot_general(pick, info, NT, preferred_element_type=F32).astype(jnp.int32)
    copy = pltpu.make_async_copy(starts_v, starts_s, sem)
    copy.start()
    k = iota((128, 256), 0)
    want = jnp.where(iota((128, 256), 1) < 128, tile, sibling)
    spread = jnp.where(k == want + 16, 32.0, jnp.where(k == want + 32, 1.0, 0.0)).astype(BF16)
    turns = jnp.dot(info, spread, preferred_element_type=F32).astype(jnp.int32) & 127

    sign = jnp.where(iota((8, WIN), 0) < 4, -1.0, 1.0)
    w[:, :WIN] = m[:, :WIN]
    for g in range(0, CHUNK, 16):
        v = m[g : g + 16, :WIN].astype(F32)
        top = pltpu.roll(v[:8], 4, 0) * sign
        low = pltpu.roll(v[8:], 4, 0) * sign
        w[g : g + 16, WIN:] = jnp.concatenate([top, low], 0).astype(BF16)
    for n in range(0, UPS, 512):
        if copies:
            copies[n // 512].wait()
        f = filt[:, :, n : n + 512].reshape(2 * WIN, 512)
        r = jnp.dot(w[...], f, preferred_element_type=F32)
        for h in range(4):
            for g in range(16):
                at = g * 128 + (n // 128 + h) * 8
                prof[at : at + 8, :] = r[8 * g : 8 * g + 8, 128 * h : 128 * h + 128]
    copy.wait()
    for which, out in enumerate((theirs, mine)):
        for g in range(16):
            for j in range(4):
                start = starts_s[1 - which, 8 * g + j]
                turn = (128 - (start & 127)) & 127
                at = g * 128 + (start >> 7) * 8 + j
                re = pltpu.roll(prof[pl.ds(at, 8, 8), :], turn, 1)
                im = pltpu.roll(prof[pl.ds(at + 4, 8, 8), :], turn, 1)
                end = pltpu.roll(prof[pl.ds(at + 64, 2, 4), :], turn, 1)
                to = g * 72 + j
                cut[which, pl.ds(to, 8, 8), :] = re
                cut[which, pl.ds(to + 4, 8, 8), :] = im
                cut[which, pl.ds(to + 64, 2, 4), :] = end
    for which, out in enumerate((theirs, mine)):
        for pair in range(8):
            done = [[], []]
            for e in range(2):
                g = 2 * pair + e
                turn = turns[8 * g : 8 * g + 8, 128 * (1 - which) : 128 * (1 - which) + 128]
                inside = lane8 + turn < 128
                parts = [cut[which, g * 72 + 8 * c : g * 72 + 8 * c + 8, :] for c in range(9)]
                done[e] = [jnp.where(inside, parts[c], parts[c + 1]) for c in range(8)]
                meta = info[8 * g : 8 * g + 8].astype(F32)
                done[e].append(
                    jnp.where(lane8 == 0, parts[8], jnp.where(lane8 < 4, meta, 0.0))
                )
            for c in range(9):
                v = jnp.concatenate([done[0][c], done[1][c]], 0).astype(BF16)
                out[16 * pair : 16 * pair + 16, 128 * c : 128 * c + 128] = v


def positions():
    tile = lax.axis_index("tile")
    core = lax.rem(tile, 2)
    x = lax.rem(tile // 2, 4)
    y = tile // 8 * 2 + lax.rem(lax.axis_index("pulse"), 2)
    own = jnp.where(core == 0, x, y)
    other = jnp.where(core == 0, y, x)
    return [core * 4 + lax.rem(own + 4 - k, 4) for k in STEPS] + [
        (1 - core) * 4 + lax.rem(other + 4 - k, 4) for k in STEPS
    ]


def gradient_kernel(*refs):
    parts = refs[:8]
    g_out, meta_out, b = refs[8:11]
    place = refs[11]
    for i, part in enumerate(parts):
        b[CHUNK * i : CHUNK * (i + 1), :] = part[...]
    row8 = iota((8, 128), 0)
    lane8 = iota((8, 128), 1)
    pick = jnp.where(
        row8 == 0,
        jnp.where(lane8 == 1, 1.0, 0.0),
        jnp.where(row8 == 1, jnp.where(lane8 == 2, 32.0, jnp.where(lane8 == 3, 1.0, 0.0)), 0.0),
    ).astype(BF16)
    meta = lax.dot_general(pick, b[:, WIN:], NT, preferred_element_type=F32)
    for i in range(8):
        meta_out[0, i : i + 1, :] = meta[0:1, CHUNK * i : CHUNK * (i + 1)]
        meta_out[1, i : i + 1, :] = meta[1:2, CHUNK * i : CHUNK * (i + 1)]
    shift = meta[0:1] * 0.0625
    keep = jnp.where((iota((8, WIN), 1) & 7) == iota((8, WIN), 0), 1.0, 0.0)
    lhs = jnp.concatenate([keep, keep * shift], 0).astype(BF16)
    sums = jnp.dot(lhs, b[...], preferred_element_type=F32)
    s = sums[:8]
    t = sums[8:]
    inner = iota((8, BW), 1) < WIN
    x0 = s + pltpu.roll(t, BW - 1, 1) - t
    dr = pltpu.roll(s, BW - 1, 1) - s
    a = jnp.where(inner, 4.0 * x0 + 1.5 * dr, 0.0)
    d = jnp.where(inner, 1.5 * x0 + 0.875 * dr, 0.0)
    p = a - d + pltpu.roll(d, 1, 1)
    q = pltpu.roll(a, 1, 1) - a
    both = jnp.concatenate([p, q], 0)
    high = both.astype(BF16)
    low = (both - high.astype(F32)).astype(BF16)
    g = lax.dot_general(jnp.concatenate([high, low], 0), b[...], NT, preferred_element_type=F32)
    g = g[:16] + g[16:]
    g = g[:8] + g[8:] * shift
    j = iota((8, WIN), 1) & 3
    row = iota((8, WIN), 0)
    by_re = jnp.sum(jnp.where(row == j, g, 0.0), axis=0, keepdims=True)
    by_im = jnp.sum(jnp.where(row == j + 4, g, 0.0), axis=0, keepdims=True)
    even = (iota((1, WIN), 1) & 4) == 0
    swapped = jnp.where(even, pltpu.roll(by_im, WIN - 4, 1), -pltpu.roll(by_im, 4, 1))
    grads = by_re + swapped
    for i, at in enumerate(positions()):
        place[pl.ds(at, 1), :] = grads[:, CHUNK * i : CHUNK * (i + 1)]
    for t in range(16):
        g_out[t] = place[...]


def image_kernel(g_in, meta, b, out_h, total, lhs, xd, out, sems):
    total[...] = jnp.sum(g_in[...], axis=0)
    even8 = (iota((8, 128), 1) & 4) == 0
    local = jnp.concatenate([total[pl.ds(at, 1), :] for at in positions()], 0)
    g_re = jnp.where(even8, local, pltpu.roll(local, 4, 1))
    g_im = jnp.where(even8, pltpu.roll(local, 124, 1), local)
    inv = (512.0**-0.5) / jnp.sqrt(g_re * g_re + g_im * g_im + 1.0)
    c_re = jnp.where(even8, g_re, g_im) * inv
    c_im = jnp.where(even8, -g_im, g_re) * inv

    def wide(v):
        return jnp.concatenate([v[i : i + 1] for i in range(8)], 1)

    shift = wide(meta[0]) * 0.0625
    dop = wide(meta[1].astype(jnp.int32))
    c_re = wide(c_re)
    c_im = wide(c_im)
    pulse = lax.axis_index("pulse")
    step = 2.0 * jnp.pi / 1024.0
    coarse = (((iota((16, WIN), 0) * 8 + pulse * ROWS) * dop) & 1023).astype(F32) * step
    finer = ((iota((8, WIN), 0) * dop) & 1023).astype(F32) * step
    cu = jnp.cos(coarse)
    su = jnp.sin(coarse)
    cv = jnp.cos(finer)
    sv = jnp.sin(finer)
    vr = cv * c_re - sv * c_im
    vi = cv * c_im + sv * c_re
    for u in range(0, 16, 2):
        pair = []
        for e in range(2):
            ur = cu[u + e : u + e + 1]
            ui = su[u + e : u + e + 1]
            pair.append((ur * vr - ui * vi, ur * vi + ui * vr))
        at = 8 * u
        for z in range(2):
            v = jnp.concatenate([pair[0][z], pair[1][z]], 0)
            lhs[at + 128 * z : at + 128 * z + 16, :] = v.astype(BF16)
            lhs[at + 256 + 128 * z : at + 272 + 128 * z, :] = (v * shift).astype(BF16)
    uv = jnp.dot(lhs[...], b[...], preferred_element_type=F32)
    diff = pltpu.roll(uv, BW - 1, 1) - uv
    xd[:, :WIN] = (uv[:256] + diff[256:])[:, :WIN].astype(BF16)
    xd[:, WIN:] = diff[:256, :WIN].astype(BF16)
    k = iota((256, 512), 0)
    col = iota((256, 512), 1)
    quarter = (col & 3).astype(F32) * 0.25
    spread = jnp.where((k & 127) == (col >> 2), jnp.where(k < 128, 1.0, quarter), 0.0).astype(BF16)
    copies = []
    for j in range(8):
        at = 128 * j
        part = jnp.concatenate([xd[:, at : at + 128], xd[:, WIN + at : WIN + at + 128]], 1)
        res = jnp.dot(part, spread, preferred_element_type=F32).astype(BF16)
        out[0, :, 512 * j : 512 * j + 512] = res[:128]
        out[1, :, 512 * j : 512 * j + 512] = res[128:]
        block = (slice(None), slice(None), pl.ds(512 * j, 512))
        copies.append(pltpu.make_async_copy(out.at[block], out_h.at[block], sems.at[j]))
        copies[-1].start()
    for copy in copies:
        copy.wait()


def vmem():
    return pl.BlockSpec(memory_space=pltpu.VMEM)


def hbm():
    return pl.BlockSpec(memory_space=pltpu.HBM)


def params(mib):
    return pltpu.CompilerParams(vmem_limit_bytes=mib * MIB)


def cost(flops, size):
    return pl.CostEstimate(flops=flops, bytes_accessed=size, transcendentals=0)


def shards(raw, filt, range_off, fine, dop, pulse_order, band_idx):
    own = pl.pallas_call(
        window_kernel,
        out_shape=jax.ShapeDtypeStruct((16, 8, BW), BF16),
        in_specs=[hbm()] * 6,
        out_specs=vmem(),
        scratch_shapes=[
            pltpu.SMEM((1, 4), jnp.int32),
            pltpu.SMEM((4,), jnp.int32),
            pltpu.SMEM((4,), jnp.int32),
            pltpu.SMEM((4,), jnp.int32),
            pltpu.SMEM((4, 16), jnp.int32),
            pltpu.VMEM((2, 4, UPS), BF16),
            pltpu.SemaphoreType.DMA((6,)),
        ],
        compiler_params=params(60),
    )(pulse_order, range_off, fine, dop, band_idx.T, raw)
    plane = lax.all_to_all(
        own, AXES, split_axis=0, concat_axis=0, axis_index_groups=planes(), tiled=True
    ).reshape(CHUNK, BW)
    chunks = [plane] + [lax.ppermute(plane, AXES, along_last(k)) for k in STEPS[1:]]
    band = jax.ShapeDtypeStruct((CHUNK, BW), BF16)
    scratch = [
        pltpu.VMEM((CHUNK, 2 * WIN), BF16),
        pltpu.VMEM((2048, 128), F32),
        pltpu.VMEM((2, 16 * 72, 128), F32),
        pltpu.VMEM((8, 128), jnp.int32),
        pltpu.SMEM((8, 128), jnp.int32),
        pltpu.SemaphoreType.DMA,
    ]
    first_bands = pl.pallas_call(
        first_band_kernel,
        out_shape=[band, band, jax.ShapeDtypeStruct(filt.shape, BF16)],
        in_specs=[vmem(), hbm()],
        out_specs=[vmem()] * 3,
        scratch_shapes=scratch + [pltpu.SemaphoreType.DMA((4,))],
        compiler_params=params(FIRST),
        cost_estimate=cost(2 * CHUNK * UPS * UPS, 8 * MIB),
    )
    bands = pl.pallas_call(
        band_kernel,
        out_shape=[band, band],
        in_specs=[vmem()] * 2,
        out_specs=[vmem()] * 2,
        scratch_shapes=scratch,
        compiler_params=params(12),
        cost_estimate=cost(2 * CHUNK * UPS * UPS, 8 * MIB),
    )
    mine = []
    given = []
    filt_v = None
    for chunk in chunks:
        if filt_v is None:
            theirs, ours, filt_v = first_bands(chunk, filt)
        else:
            theirs, ours = bands(chunk, filt_v)
        mine.append(ours)
        given.append(lax.ppermute(theirs, AXES, other_core()))
    partial, meta, b = pl.pallas_call(
        gradient_kernel,
        out_shape=[
            jax.ShapeDtypeStruct((16, 8, 128), F32),
            jax.ShapeDtypeStruct((2, 8, 128), F32),
            jax.ShapeDtypeStruct((WIN, BW), BF16),
        ],
        in_specs=[vmem()] * 8,
        out_specs=[vmem()] * 3,
        scratch_shapes=[pltpu.VMEM((8, 128), F32)],
        compiler_params=params(12),
    )(*mine, *given)
    grads = lax.all_to_all(partial, "tile", split_axis=0, concat_axis=0, tiled=True)
    return pl.pallas_call(
        image_kernel,
        out_shape=jax.ShapeDtypeStruct((2, ROWS, 4 * WIN), BF16),
        in_specs=[vmem()] * 3,
        out_specs=hbm(),
        scratch_shapes=[
            pltpu.VMEM((8, 128), F32),
            pltpu.VMEM((512, WIN), BF16),
            pltpu.VMEM((256, 2 * WIN), BF16),
            pltpu.VMEM((2, ROWS, 4 * WIN), BF16),
            pltpu.SemaphoreType.DMA((8,)),
        ],
        compiler_params=params(20),
    )(grads, meta, b)


def solution(mesh):
    return jax.shard_map(
        shards,
        mesh=mesh,
        in_specs=(
            P(None, AXES, None),
            P(),
            P(AXES),
            P(AXES),
            P(AXES),
            P(AXES, None),
            P(None, AXES),
        ),
        out_specs=P(None, "pulse", "tile"),
        check_vma=False,
    )
```

```python
import jax
import jax.numpy as jnp
from jax import lax
from jax.experimental import pallas as pl
from jax.experimental.pallas import tpu as pltpu
from jax.sharding import PartitionSpec as P

AXES = ("pulse", "tile")
WIN = 1024
UPS = 2048
BW = WIN + 128
ROWS = 128
CHUNK = 128
EARLY = 7 * CHUNK
STEPS = (0, 1, 3, 2)
F32 = jnp.float32
BF16 = jnp.bfloat16
NT = (((1,), (1,)), ((), ()))
MIB = 1024 * 1024
FIRST = 42


def linear(z, y, x, core):
    return (z * 2 + y % 2) * 16 + ((y // 2) * 4 + x) * 2 + core


PLACES = [(z, y, x, c) for z in range(4) for y in range(4) for x in range(4) for c in range(2)]


def planes():
    groups = {}
    for z, y, x, c in PLACES:
        groups.setdefault((c, x if c == 0 else y), []).append(linear(z, y, x, c))
    return [groups[key] for key in sorted(groups)]


def along_last(k):
    return [
        (
            linear(z, y, x, c),
            linear(z, y, (x + k) % 4, c) if c == 0 else linear(z, (y + k) % 4, x, c),
        )
        for z, y, x, c in PLACES
    ]


def other_core():
    return [(linear(z, y, x, c), linear(z, y, x, 1 - c)) for z, y, x, c in PLACES]


def near():
    groups = {}
    for z, y, x, c in PLACES:
        groups.setdefault((z, y in (0, 3), c), []).append(linear(z, y, x, c))
    return [groups[key] for key in sorted(groups)]


def iota(shape, axis):
    return lax.broadcasted_iota(jnp.int32, shape, axis)


def window_kernel(order_h, off_h, fine_h, dop_h, band_h, raw_h, out, order, off, fine, dop, band, raw, sems):
    pairs = ((order_h, order), (off_h, off), (fine_h, fine), (dop_h, dop), (band_h, band), (raw_h, raw))
    copies = [pltpu.make_async_copy(a, b, sems.at[i]) for i, (a, b) in enumerate(pairs)]
    for copy in copies:
        copy.start()
    for copy in copies:
        copy.wait()
    x = jnp.concatenate([raw[0].astype(F32), raw[1].astype(F32)], 0)
    row = iota((8, WIN), 0)
    lane = iota((1, 128), 1)
    meta_row = iota((8, 128), 0)
    both = jnp.zeros((8, WIN), F32)
    meta = jnp.zeros((8, 128), jnp.int32)
    for j in range(4):
        k = order[0, j]
        y = pltpu.roll(x, lax.rem(UPS - off[k], UPS), 1)[:, :WIN]
        one_re = jnp.sum(jnp.where(row == k, y, 0.0), axis=0, keepdims=True)
        one_im = jnp.sum(jnp.where(row == k + 4, y, 0.0), axis=0, keepdims=True)
        both = jnp.where(row == j, one_re, jnp.where(row == j + 4, one_im, both))
        d = dop[k]
        v = jnp.where(lane == 1, fine[k], 0)
        v = jnp.where(lane == 2, d >> 5, v)
        v = jnp.where(lane == 3, d & 31, v)
        for t in range(16):
            b = band[k, t]
            v = jnp.where(lane == 16 + t, b >> 5, v)
            v = jnp.where(lane == 32 + t, b & 31, v)
        meta = jnp.where((meta_row & 3) == j, v, meta)
    both = both.astype(BF16)
    meta = meta.astype(F32).astype(BF16)
    for i in range(16):
        out[i, :, :WIN] = both
        out[i, :, WIN:] = meta


def first_band_kernel(m, filt_h, theirs, mine, filt, w, prof, cut, starts_v, starts_s, sem, sems):
    copies = []
    for i in range(4):
        block = (slice(None), slice(None), pl.ds(512 * i, 512))
        copies.append(pltpu.make_async_copy(filt_h.at[block], filt.at[block], sems.at[i]))
        copies[-1].start()
    band_kernel(m, filt, theirs, mine, w, prof, cut, starts_v, starts_s, sem, copies)


def band_kernel(m, filt, theirs, mine, w, prof, cut, starts_v, starts_s, sem, copies=None):
    tile = lax.axis_index("tile")
    sibling = tile + 1 - 2 * lax.rem(tile, 2)
    lane8 = iota((8, 128), 1)
    row8 = iota((8, 128), 0)
    info = m[:, WIN:]
    want = jnp.where(row8 == 0, tile, sibling)
    pick = jnp.where(lane8 == want + 16, 32.0, jnp.where(lane8 == want + 32, 1.0, 0.0)).astype(BF16)
    starts_v[...] = lax.dot_general(pick, info, NT, preferred_element_type=F32).astype(jnp.int32)
    copy = pltpu.make_async_copy(starts_v, starts_s, sem)
    copy.start()
    k = iota((128, 256), 0)
    want = jnp.where(iota((128, 256), 1) < 128, tile, sibling)
    spread = jnp.where(k == want + 16, 32.0, jnp.where(k == want + 32, 1.0, 0.0)).astype(BF16)
    turns = jnp.dot(info, spread, preferred_element_type=F32).astype(jnp.int32) & 127

    sign = jnp.where(iota((8, WIN), 0) < 4, -1.0, 1.0)
    w[:, :WIN] = m[:, :WIN]
    for g in range(0, CHUNK, 16):
        v = m[g : g + 16, :WIN].astype(F32)
        top = pltpu.roll(v[:8], 4, 0) * sign
        low = pltpu.roll(v[8:], 4, 0) * sign
        w[g : g + 16, WIN:] = jnp.concatenate([top, low], 0).astype(BF16)
    for n in range(0, UPS, 512):
        if copies:
            copies[n // 512].wait()
        f = filt[:, :, n : n + 512].reshape(2 * WIN, 512)
        r = jnp.dot(w[...], f, preferred_element_type=F32)
        for h in range(4):
            for g in range(16):
                at = g * 128 + (n // 128 + h) * 8
                prof[at : at + 8, :] = r[8 * g : 8 * g + 8, 128 * h : 128 * h + 128]
    copy.wait()
    for which, out in enumerate((theirs, mine)):
        for g in range(16):
            for j in range(4):
                start = starts_s[1 - which, 8 * g + j]
                turn = (128 - (start & 127)) & 127
                at = g * 128 + (start >> 7) * 8 + j
                re = pltpu.roll(prof[pl.ds(at, 8, 8), :], turn, 1)
                im = pltpu.roll(prof[pl.ds(at + 4, 8, 8), :], turn, 1)
                end = pltpu.roll(prof[pl.ds(at + 64, 2, 4), :], turn, 1)
                to = g * 72 + j
                cut[which, pl.ds(to, 8, 8), :] = re
                cut[which, pl.ds(to + 4, 8, 8), :] = im
                cut[which, pl.ds(to + 64, 2, 4), :] = end
    for which, out in enumerate((theirs, mine)):
        for pair in range(8):
            done = [[], []]
            for e in range(2):
                g = 2 * pair + e
                turn = turns[8 * g : 8 * g + 8, 128 * (1 - which) : 128 * (1 - which) + 128]
                inside = lane8 + turn < 128
                parts = [cut[which, g * 72 + 8 * c : g * 72 + 8 * c + 8, :] for c in range(9)]
                done[e] = [jnp.where(inside, parts[c], parts[c + 1]) for c in range(8)]
                meta = info[8 * g : 8 * g + 8].astype(F32)
                done[e].append(
                    jnp.where(lane8 == 0, parts[8], jnp.where(lane8 < 4, meta, 0.0))
                )
            for c in range(9):
                v = jnp.concatenate([done[0][c], done[1][c]], 0).astype(BF16)
                out[16 * pair : 16 * pair + 16, 128 * c : 128 * c + 128] = v


def positions():
    tile = lax.axis_index("tile")
    core = lax.rem(tile, 2)
    x = lax.rem(tile // 2, 4)
    y = tile // 8 * 2 + lax.rem(lax.axis_index("pulse"), 2)
    own = jnp.where(core == 0, x, y)
    other = jnp.where(core == 0, y, x)
    return [core * 4 + lax.rem(own + 4 - k, 4) for k in STEPS] + [
        (1 - core) * 4 + lax.rem(other + 4 - k, 4) for k in STEPS
    ]


def lane_info(b):
    row8 = iota((8, 128), 0)
    lane8 = iota((8, 128), 1)
    pick = jnp.where(
        row8 == 0,
        jnp.where(lane8 == 1, 1.0, 0.0),
        jnp.where(row8 == 1, jnp.where(lane8 == 2, 32.0, jnp.where(lane8 == 3, 1.0, 0.0)), 0.0),
    ).astype(BF16)
    return lax.dot_general(pick, b, NT, preferred_element_type=F32)


def block_rows(shift):
    size = shift.shape[1]
    keep = jnp.where((iota((8, size), 1) & 7) == iota((8, size), 0), 1.0, 0.0)
    return jnp.concatenate([keep, keep * shift], 0).astype(BF16)


def sum_kernel(*refs):
    parts = refs[:7]
    sums, info, b = refs[7:]
    for i, part in enumerate(parts):
        b[CHUNK * i : CHUNK * (i + 1), :] = part[...]
    b[EARLY:, :] = jnp.zeros((CHUNK, BW), BF16)
    info[...] = lane_info(b[:EARLY, WIN:])
    lhs = block_rows(info[0:1] * 0.0625)
    sums[...] = jnp.dot(lhs, b[:EARLY], preferred_element_type=F32)


def gradient_kernel(last, early, info, b_in, g_out, meta_out, b, place):
    b[EARLY:, :] = last[...]
    late = lane_info(last[:, WIN:])
    meta = jnp.concatenate([info[0:2], late[0:2]], 1)
    for i in range(8):
        for e in range(2):
            meta_out[e, i : i + 1, :] = meta[e : e + 1, CHUNK * i : CHUNK * (i + 1)]
    shift = meta[0:1] * 0.0625
    sums = early[...] + jnp.dot(block_rows(late[0:1] * 0.0625), last[...], preferred_element_type=F32)
    s = sums[:8]
    t = sums[8:]
    inner = iota((8, BW), 1) < WIN
    x0 = s + pltpu.roll(t, BW - 1, 1) - t
    dr = pltpu.roll(s, BW - 1, 1) - s
    a = jnp.where(inner, 4.0 * x0 + 1.5 * dr, 0.0)
    d = jnp.where(inner, 1.5 * x0 + 0.875 * dr, 0.0)
    p = a - d + pltpu.roll(d, 1, 1)
    q = pltpu.roll(a, 1, 1) - a
    both = jnp.concatenate([p, q], 0)
    high = both.astype(BF16)
    low = (both - high.astype(F32)).astype(BF16)
    lhs = jnp.concatenate([high, low], 0)
    g = jnp.concatenate(
        [
            lax.dot_general(lhs, b_in[:EARLY], NT, preferred_element_type=F32),
            lax.dot_general(lhs, last[...], NT, preferred_element_type=F32),
        ],
        1,
    )
    g = g[:16] + g[16:]
    g = g[:8] + g[8:] * shift
    j = iota((8, WIN), 1) & 3
    row = iota((8, WIN), 0)
    by_re = jnp.sum(jnp.where(row == j, g, 0.0), axis=0, keepdims=True)
    by_im = jnp.sum(jnp.where(row == j + 4, g, 0.0), axis=0, keepdims=True)
    even = (iota((1, WIN), 1) & 4) == 0
    swapped = jnp.where(even, pltpu.roll(by_im, WIN - 4, 1), -pltpu.roll(by_im, 4, 1))
    grads = by_re + swapped
    for i, at in enumerate(positions()):
        place[pl.ds(at, 1), :] = grads[:, CHUNK * i : CHUNK * (i + 1)]
    for t in range(8):
        g_out[t] = place[...]


def turn(m):
    quadrant = (m + 128) >> 8
    p = (m - (quadrant << 8)).astype(F32) * (2.0 * jnp.pi / 1024.0)
    p2 = p * p
    c = 1.0 + p2 * (-1.0 / 2 + p2 * (1.0 / 24 + p2 * (-1.0 / 720 + p2 * (1.0 / 40320))))
    s = p * (1.0 + p2 * (-1.0 / 6 + p2 * (1.0 / 120 + p2 * (-1.0 / 5040 + p2 * (1.0 / 362880)))))
    odd = (quadrant & 1) == 1
    cos = jnp.where(odd, s, c)
    sin = jnp.where(odd, c, s)
    cos = jnp.where(((quadrant + 1) & 2) == 2, -cos, cos)
    sin = jnp.where((quadrant & 2) == 2, -sin, sin)
    return cos, sin


def image_kernel(g_in, g_other, meta, b, out_h, total, lhs, xd, out, sems):
    total[...] = jnp.sum(g_in[...], axis=0) + jnp.sum(g_other[...], axis=0)
    even8 = (iota((8, 128), 1) & 4) == 0
    local = jnp.concatenate([total[pl.ds(at, 1), :] for at in positions()], 0)
    g_re = jnp.where(even8, local, pltpu.roll(local, 4, 1))
    g_im = jnp.where(even8, pltpu.roll(local, 124, 1), local)
    inv = (512.0**-0.5) / jnp.sqrt(g_re * g_re + g_im * g_im + 1.0)
    c_re = jnp.where(even8, g_re, g_im) * inv
    c_im = jnp.where(even8, -g_im, g_re) * inv

    def wide(v):
        return jnp.concatenate([v[i : i + 1] for i in range(8)], 1)

    shift = wide(meta[0]) * 0.0625
    dop = wide(meta[1].astype(jnp.int32))
    c_re = wide(c_re)
    c_im = wide(c_im)
    pulse = lax.axis_index("pulse")
    cu, su = turn(((iota((16, WIN), 0) * 8 + pulse * ROWS) * dop) & 1023)
    cv, sv = turn((iota((8, WIN), 0) * dop) & 1023)
    vr = cv * c_re - sv * c_im
    vi = cv * c_im + sv * c_re
    for u in range(0, 16, 2):
        pair = []
        for e in range(2):
            ur = cu[u + e : u + e + 1]
            ui = su[u + e : u + e + 1]
            pair.append((ur * vr - ui * vi, ur * vi + ui * vr))
        at = 8 * u
        for z in range(2):
            v = jnp.concatenate([pair[0][z], pair[1][z]], 0)
            lhs[at + 128 * z : at + 128 * z + 16, :] = v.astype(BF16)
            lhs[at + 256 + 128 * z : at + 272 + 128 * z, :] = (v * shift).astype(BF16)
    uv = jnp.dot(lhs[...], b[...], preferred_element_type=F32)
    diff = pltpu.roll(uv, BW - 1, 1) - uv
    xd[:, :WIN] = (uv[:256] + diff[256:])[:, :WIN].astype(BF16)
    xd[:, WIN:] = diff[:256, :WIN].astype(BF16)
    k = iota((256, 512), 0)
    col = iota((256, 512), 1)
    quarter = (col & 3).astype(F32) * 0.25
    spread = jnp.where((k & 127) == (col >> 2), jnp.where(k < 128, 1.0, quarter), 0.0).astype(BF16)
    copies = []
    for j in range(8):
        at = 128 * j
        part = jnp.concatenate([xd[:, at : at + 128], xd[:, WIN + at : WIN + at + 128]], 1)
        res = jnp.dot(part, spread, preferred_element_type=F32).astype(BF16)
        out[0, :, 512 * j : 512 * j + 512] = res[:128]
        out[1, :, 512 * j : 512 * j + 512] = res[128:]
        block = (slice(None), slice(None), pl.ds(512 * j, 512))
        copies.append(pltpu.make_async_copy(out.at[block], out_h.at[block], sems.at[j]))
        copies[-1].start()
    for copy in copies:
        copy.wait()


def vmem():
    return pl.BlockSpec(memory_space=pltpu.VMEM)


def hbm():
    return pl.BlockSpec(memory_space=pltpu.HBM)


def params(mib):
    return pltpu.CompilerParams(vmem_limit_bytes=mib * MIB)


def cost(flops, size):
    return pl.CostEstimate(flops=flops, bytes_accessed=size, transcendentals=0)


def shards(raw, filt, range_off, fine, dop, pulse_order, band_idx):
    own = pl.pallas_call(
        window_kernel,
        out_shape=jax.ShapeDtypeStruct((16, 8, BW), BF16),
        in_specs=[hbm()] * 6,
        out_specs=vmem(),
        scratch_shapes=[
            pltpu.SMEM((1, 4), jnp.int32),
            pltpu.SMEM((4,), jnp.int32),
            pltpu.SMEM((4,), jnp.int32),
            pltpu.SMEM((4,), jnp.int32),
            pltpu.SMEM((4, 16), jnp.int32),
            pltpu.VMEM((2, 4, UPS), BF16),
            pltpu.SemaphoreType.DMA((6,)),
        ],
        compiler_params=params(60),
    )(pulse_order, range_off, fine, dop, band_idx.T, raw)
    plane = lax.all_to_all(
        own, AXES, split_axis=0, concat_axis=0, axis_index_groups=planes(), tiled=True
    ).reshape(CHUNK, BW)
    chunks = [plane] + [lax.ppermute(plane, AXES, along_last(k)) for k in STEPS[1:]]
    band = jax.ShapeDtypeStruct((CHUNK, BW), BF16)
    scratch = [
        pltpu.VMEM((CHUNK, 2 * WIN), BF16),
        pltpu.VMEM((2048, 128), F32),
        pltpu.VMEM((2, 16 * 72, 128), F32),
        pltpu.VMEM((8, 128), jnp.int32),
        pltpu.SMEM((8, 128), jnp.int32),
        pltpu.SemaphoreType.DMA,
    ]
    first_bands = pl.pallas_call(
        first_band_kernel,
        out_shape=[band, band, jax.ShapeDtypeStruct(filt.shape, BF16)],
        in_specs=[vmem(), hbm()],
        out_specs=[vmem()] * 3,
        scratch_shapes=scratch + [pltpu.SemaphoreType.DMA((4,))],
        compiler_params=params(FIRST),
        cost_estimate=cost(2 * CHUNK * UPS * UPS, 8 * MIB),
    )
    bands = pl.pallas_call(
        band_kernel,
        out_shape=[band, band],
        in_specs=[vmem()] * 2,
        out_specs=[vmem()] * 2,
        scratch_shapes=scratch,
        compiler_params=params(12),
        cost_estimate=cost(2 * CHUNK * UPS * UPS, 8 * MIB),
    )
    mine = []
    given = []
    filt_v = None
    for chunk in chunks:
        if filt_v is None:
            theirs, ours, filt_v = first_bands(chunk, filt)
        else:
            theirs, ours = bands(chunk, filt_v)
        mine.append(ours)
        given.append(lax.ppermute(theirs, AXES, other_core()))
    sums, info, early = pl.pallas_call(
        sum_kernel,
        out_shape=[
            jax.ShapeDtypeStruct((16, BW), F32),
            jax.ShapeDtypeStruct((8, EARLY), F32),
            jax.ShapeDtypeStruct((WIN, BW), BF16),
        ],
        in_specs=[vmem()] * 7,
        out_specs=[vmem()] * 3,
        compiler_params=params(12),
        cost_estimate=cost(2 * 16 * EARLY * BW, 4 * MIB),
    )(*mine, *given[:3])
    partial, meta, b = pl.pallas_call(
        gradient_kernel,
        out_shape=[
            jax.ShapeDtypeStruct((8, 8, 128), F32),
            jax.ShapeDtypeStruct((2, 8, 128), F32),
            jax.ShapeDtypeStruct((WIN, BW), BF16),
        ],
        in_specs=[vmem()] * 4,
        out_specs=[vmem()] * 3,
        scratch_shapes=[pltpu.VMEM((8, 128), F32)],
        input_output_aliases={3: 2},
        compiler_params=params(12),
    )(given[3], sums, info, early)
    grads = lax.all_to_all(
        partial, AXES, split_axis=0, concat_axis=0, axis_index_groups=near(), tiled=True
    )
    others = lax.ppermute(grads, AXES, other_core())
    return pl.pallas_call(
        image_kernel,
        out_shape=jax.ShapeDtypeStruct((2, ROWS, 4 * WIN), BF16),
        in_specs=[vmem()] * 4,
        out_specs=hbm(),
        scratch_shapes=[
            pltpu.VMEM((8, 128), F32),
            pltpu.VMEM((512, WIN), BF16),
            pltpu.VMEM((256, 2 * WIN), BF16),
            pltpu.VMEM((2, ROWS, 4 * WIN), BF16),
            pltpu.SemaphoreType.DMA((8,)),
        ],
        compiler_params=params(20),
    )(grads, others, meta, b)


def solution(mesh):
    return jax.shard_map(
        shards,
        mesh=mesh,
        in_specs=(
            P(None, AXES, None),
            P(),
            P(AXES),
            P(AXES),
            P(AXES),
            P(AXES, None),
            P(None, AXES),
        ),
        out_specs=P(None, "pulse", "tile"),
        check_vma=False,
    )
```

```python
import functools

import jax
import jax.numpy as jnp
from jax import lax
from jax.experimental import pallas as pl
from jax.experimental.pallas import tpu as pltpu
from jax.sharding import PartitionSpec as P

AXES = ("pulse", "tile")
WIN = 1024
UPS = 2048
BW = WIN + 128
ROWS = 128
CHUNK = 128
EARLY = 7 * CHUNK
STEPS = (0, 1, 3, 2)
F32 = jnp.float32
BF16 = jnp.bfloat16
NT = (((1,), (1,)), ((), ()))
MIB = 1024 * 1024
FIRST = 42


def linear(z, y, x, core):
    return (z * 2 + y % 2) * 16 + ((y // 2) * 4 + x) * 2 + core


PLACES = [(z, y, x, c) for z in range(4) for y in range(4) for x in range(4) for c in range(2)]


def planes():
    groups = {}
    for z, y, x, c in PLACES:
        groups.setdefault((c, x if c == 0 else y), []).append(linear(z, y, x, c))
    return [groups[key] for key in sorted(groups)]


def along_last(k):
    return [
        (
            linear(z, y, x, c),
            linear(z, y, (x + k) % 4, c) if c == 0 else linear(z, (y + k) % 4, x, c),
        )
        for z, y, x, c in PLACES
    ]


def other_core():
    return [(linear(z, y, x, c), linear(z, y, x, 1 - c)) for z, y, x, c in PLACES]


def iota(shape, axis):
    return lax.broadcasted_iota(jnp.int32, shape, axis)


def window_kernel(order_h, off_h, fine_h, dop_h, band_h, raw_h, out, order, off, fine, dop, band, raw, sems):
    pairs = ((order_h, order), (off_h, off), (fine_h, fine), (dop_h, dop), (band_h, band), (raw_h, raw))
    copies = [pltpu.make_async_copy(a, b, sems.at[i]) for i, (a, b) in enumerate(pairs)]
    for copy in copies:
        copy.start()
    for copy in copies:
        copy.wait()
    x = jnp.concatenate([raw[0].astype(F32), raw[1].astype(F32)], 0)
    row = iota((8, WIN), 0)
    lane = iota((1, 128), 1)
    meta_row = iota((8, 128), 0)
    both = jnp.zeros((8, WIN), F32)
    meta = jnp.zeros((8, 128), jnp.int32)
    for j in range(4):
        k = order[0, j]
        y = pltpu.roll(x, lax.rem(UPS - off[k], UPS), 1)[:, :WIN]
        one_re = jnp.sum(jnp.where(row == k, y, 0.0), axis=0, keepdims=True)
        one_im = jnp.sum(jnp.where(row == k + 4, y, 0.0), axis=0, keepdims=True)
        both = jnp.where(row == j, one_re, jnp.where(row == j + 4, one_im, both))
        d = dop[k]
        v = jnp.where(lane == 1, fine[k], 0)
        v = jnp.where(lane == 2, d >> 5, v)
        v = jnp.where(lane == 3, d & 31, v)
        for t in range(16):
            b = band[k, t]
            v = jnp.where(lane == 16 + t, b >> 5, v)
            v = jnp.where(lane == 32 + t, b & 31, v)
        meta = jnp.where((meta_row & 3) == j, v, meta)
    both = both.astype(BF16)
    meta = meta.astype(F32).astype(BF16)
    for i in range(16):
        out[i, :, :WIN] = both
        out[i, :, WIN:] = meta


def first_band_kernel(m, filt_h, theirs, mine, filt, w, prof, cut, starts_v, starts_s, sem, sems):
    copies = []
    for i in range(4):
        block = (slice(None), slice(None), pl.ds(512 * i, 512))
        copies.append(pltpu.make_async_copy(filt_h.at[block], filt.at[block], sems.at[i]))
        copies[-1].start()
    outs = (theirs, 0, mine, 0)
    cut_bands(m, filt, outs, (w, prof, cut, starts_v, starts_s, sem), copies)


def middle_band_kernel(index, m, filt, theirs_in, mine_in, theirs, mine, *scratch):
    cut_bands(m, filt, (theirs, CHUNK * index, mine, CHUNK * index), scratch)


def last_band_kernel(m, filt, mine_in, theirs, mine, *scratch):
    cut_bands(m, filt, (theirs, 0, mine, CHUNK * 3), scratch)


def cut_bands(m, filt, outs, scratch, copies=None):
    theirs, theirs_at, mine, mine_at = outs
    w, prof, cut, starts_v, starts_s, sem = scratch
    tile = lax.axis_index("tile")
    sibling = tile + 1 - 2 * lax.rem(tile, 2)
    lane8 = iota((8, 128), 1)
    row8 = iota((8, 128), 0)
    info = m[:, WIN:]
    want = jnp.where(row8 == 0, tile, sibling)
    pick = jnp.where(lane8 == want + 16, 32.0, jnp.where(lane8 == want + 32, 1.0, 0.0)).astype(BF16)
    starts_v[...] = lax.dot_general(pick, info, NT, preferred_element_type=F32).astype(jnp.int32)
    copy = pltpu.make_async_copy(starts_v, starts_s, sem)
    copy.start()
    k = iota((128, 256), 0)
    want = jnp.where(iota((128, 256), 1) < 128, tile, sibling)
    spread = jnp.where(k == want + 16, 32.0, jnp.where(k == want + 32, 1.0, 0.0)).astype(BF16)
    turns = jnp.dot(info, spread, preferred_element_type=F32).astype(jnp.int32) & 127

    sign = jnp.where(iota((8, WIN), 0) < 4, -1.0, 1.0)
    w[:, :WIN] = m[:, :WIN]
    for g in range(0, CHUNK, 16):
        v = m[g : g + 16, :WIN].astype(F32)
        top = pltpu.roll(v[:8], 4, 0) * sign
        low = pltpu.roll(v[8:], 4, 0) * sign
        w[g : g + 16, WIN:] = jnp.concatenate([top, low], 0).astype(BF16)
    for n in range(0, UPS, 512):
        if copies:
            copies[n // 512].wait()
        f = filt[:, :, n : n + 512].reshape(2 * WIN, 512)
        r = jnp.dot(w[...], f, preferred_element_type=F32)
        for h in range(4):
            for g in range(16):
                at = g * 128 + (n // 128 + h) * 8
                prof[at : at + 8, :] = r[8 * g : 8 * g + 8, 128 * h : 128 * h + 128]
    copy.wait()
    for which in range(2):
        for g in range(16):
            for j in range(4):
                start = starts_s[1 - which, 8 * g + j]
                turn = (128 - (start & 127)) & 127
                at = g * 128 + (start >> 7) * 8 + j
                re = pltpu.roll(prof[pl.ds(at, 8, 8), :], turn, 1)
                im = pltpu.roll(prof[pl.ds(at + 4, 8, 8), :], turn, 1)
                end = pltpu.roll(prof[pl.ds(at + 64, 2, 4), :], turn, 1)
                to = g * 72 + j
                cut[which, pl.ds(to, 8, 8), :] = re
                cut[which, pl.ds(to + 4, 8, 8), :] = im
                cut[which, pl.ds(to + 64, 2, 4), :] = end
    for which, (out, to) in enumerate(((theirs, theirs_at), (mine, mine_at))):
        for pair in range(8):
            done = [[], []]
            for e in range(2):
                g = 2 * pair + e
                turn = turns[8 * g : 8 * g + 8, 128 * (1 - which) : 128 * (1 - which) + 128]
                inside = lane8 + turn < 128
                parts = [cut[which, g * 72 + 8 * c : g * 72 + 8 * c + 8, :] for c in range(9)]
                done[e] = [jnp.where(inside, parts[c], parts[c + 1]) for c in range(8)]
                meta = info[8 * g : 8 * g + 8].astype(F32)
                done[e].append(
                    jnp.where(lane8 == 0, parts[8], jnp.where(lane8 < 4, meta, 0.0))
                )
            for c in range(9):
                v = jnp.concatenate([done[0][c], done[1][c]], 0).astype(BF16)
                at = to + 16 * pair
                out[at : at + 16, 128 * c : 128 * c + 128] = v


def positions():
    tile = lax.axis_index("tile")
    core = lax.rem(tile, 2)
    x = lax.rem(tile // 2, 4)
    y = tile // 8 * 2 + lax.rem(lax.axis_index("pulse"), 2)
    own = jnp.where(core == 0, x, y)
    other = jnp.where(core == 0, y, x)
    return [core * 4 + lax.rem(own + 4 - k, 4) for k in STEPS] + [
        (1 - core) * 4 + lax.rem(other + 4 - k, 4) for k in STEPS
    ]


def lane_info(b):
    row8 = iota((8, 128), 0)
    lane8 = iota((8, 128), 1)
    pick = jnp.where(
        row8 == 0,
        jnp.where(lane8 == 1, 1.0, 0.0),
        jnp.where(row8 == 1, jnp.where(lane8 == 2, 32.0, jnp.where(lane8 == 3, 1.0, 0.0)), 0.0),
    ).astype(BF16)
    return lax.dot_general(pick, b, NT, preferred_element_type=F32)


def block_rows(shift):
    size = shift.shape[1]
    keep = jnp.where((iota((8, size), 1) & 7) == iota((8, size), 0), 1.0, 0.0)
    return jnp.concatenate([keep, keep * shift], 0).astype(BF16)


def sum_kernel(given, b_in, sums, info, b):
    b[4 * CHUNK : EARLY, :] = given[...]
    halves = ((b_in, 0, 4 * CHUNK), (given, 4 * CHUNK, EARLY))
    for part, low, high in halves:
        info[:, low:high] = lane_info(part[: high - low, WIN:])
    total = jnp.zeros((16, BW), F32)
    for part, low, high in halves:
        lhs = block_rows(info[0:1, low:high] * 0.0625)
        total += jnp.dot(lhs, part[: high - low], preferred_element_type=F32)
    sums[...] = total


def gradient_kernel(last, early, info, b_in, g_out, meta_out, b, place):
    b[EARLY:, :] = last[...]
    late = lane_info(last[:, WIN:])
    meta = jnp.concatenate([info[0:2], late[0:2]], 1)
    for i in range(8):
        for e in range(2):
            meta_out[e, i : i + 1, :] = meta[e : e + 1, CHUNK * i : CHUNK * (i + 1)]
    shift = meta[0:1] * 0.0625
    sums = early[...] + jnp.dot(block_rows(late[0:1] * 0.0625), last[...], preferred_element_type=F32)
    s = sums[:8]
    t = sums[8:]
    inner = iota((8, BW), 1) < WIN
    x0 = s + pltpu.roll(t, BW - 1, 1) - t
    dr = pltpu.roll(s, BW - 1, 1) - s
    a = jnp.where(inner, 4.0 * x0 + 1.5 * dr, 0.0)
    d = jnp.where(inner, 1.5 * x0 + 0.875 * dr, 0.0)
    p = a - d + pltpu.roll(d, 1, 1)
    q = pltpu.roll(a, 1, 1) - a
    both = jnp.concatenate([p, q], 0)
    high = both.astype(BF16)
    low = (both - high.astype(F32)).astype(BF16)
    lhs = jnp.concatenate([high, low], 0)
    g = jnp.concatenate(
        [
            lax.dot_general(lhs, b_in[:EARLY], NT, preferred_element_type=F32),
            lax.dot_general(lhs, last[...], NT, preferred_element_type=F32),
        ],
        1,
    )
    g = g[:16] + g[16:]
    g = g[:8] + g[8:] * shift
    j = iota((8, WIN), 1) & 3
    row = iota((8, WIN), 0)
    by_re = jnp.sum(jnp.where(row == j, g, 0.0), axis=0, keepdims=True)
    by_im = jnp.sum(jnp.where(row == j + 4, g, 0.0), axis=0, keepdims=True)
    even = (iota((1, WIN), 1) & 4) == 0
    swapped = jnp.where(even, pltpu.roll(by_im, WIN - 4, 1), -pltpu.roll(by_im, 4, 1))
    grads = by_re + swapped
    for i, at in enumerate(positions()):
        place[pl.ds(at, 1), :] = grads[:, CHUNK * i : CHUNK * (i + 1)]
    for t in range(16):
        g_out[t] = place[...]


def turn(m):
    quadrant = (m + 128) >> 8
    p = (m - (quadrant << 8)).astype(F32) * (2.0 * jnp.pi / 1024.0)
    p2 = p * p
    c = 1.0 + p2 * (-1.0 / 2 + p2 * (1.0 / 24 + p2 * (-1.0 / 720 + p2 * (1.0 / 40320))))
    s = p * (1.0 + p2 * (-1.0 / 6 + p2 * (1.0 / 120 + p2 * (-1.0 / 5040 + p2 * (1.0 / 362880)))))
    odd = (quadrant & 1) == 1
    cos = jnp.where(odd, s, c)
    sin = jnp.where(odd, c, s)
    cos = jnp.where(((quadrant + 1) & 2) == 2, -cos, cos)
    sin = jnp.where((quadrant & 2) == 2, -sin, sin)
    return cos, sin


def image_kernel(g_in, meta, b, out_h, total, lhs, xd, out, sems):
    total[...] = jnp.sum(g_in[...], axis=0)
    even8 = (iota((8, 128), 1) & 4) == 0
    local = jnp.concatenate([total[pl.ds(at, 1), :] for at in positions()], 0)
    g_re = jnp.where(even8, local, pltpu.roll(local, 4, 1))
    g_im = jnp.where(even8, pltpu.roll(local, 124, 1), local)
    inv = (512.0**-0.5) / jnp.sqrt(g_re * g_re + g_im * g_im + 1.0)
    c_re = jnp.where(even8, g_re, g_im) * inv
    c_im = jnp.where(even8, -g_im, g_re) * inv

    def wide(v):
        return jnp.concatenate([v[i : i + 1] for i in range(8)], 1)

    shift = wide(meta[0]) * 0.0625
    dop = wide(meta[1].astype(jnp.int32))
    c_re = wide(c_re)
    c_im = wide(c_im)
    pulse = lax.axis_index("pulse")
    cu, su = turn(((iota((16, WIN), 0) * 8 + pulse * ROWS) * dop) & 1023)
    cv, sv = turn((iota((8, WIN), 0) * dop) & 1023)
    vr = cv * c_re - sv * c_im
    vi = cv * c_im + sv * c_re
    for u in range(0, 16, 2):
        pair = []
        for e in range(2):
            ur = cu[u + e : u + e + 1]
            ui = su[u + e : u + e + 1]
            pair.append((ur * vr - ui * vi, ur * vi + ui * vr))
        at = 8 * u
        for z in range(2):
            v = jnp.concatenate([pair[0][z], pair[1][z]], 0)
            lhs[at + 128 * z : at + 128 * z + 16, :] = v.astype(BF16)
            lhs[at + 256 + 128 * z : at + 272 + 128 * z, :] = (v * shift).astype(BF16)
    uv = jnp.dot(lhs[...], b[...], preferred_element_type=F32)
    diff = pltpu.roll(uv, BW - 1, 1) - uv
    xd[:, :WIN] = (uv[:256] + diff[256:])[:, :WIN].astype(BF16)
    xd[:, WIN:] = diff[:256, :WIN].astype(BF16)
    k = iota((256, 512), 0)
    col = iota((256, 512), 1)
    quarter = (col & 3).astype(F32) * 0.25
    spread = jnp.where((k & 127) == (col >> 2), jnp.where(k < 128, 1.0, quarter), 0.0).astype(BF16)
    copies = []
    for j in range(8):
        at = 128 * j
        part = jnp.concatenate([xd[:, at : at + 128], xd[:, WIN + at : WIN + at + 128]], 1)
        res = jnp.dot(part, spread, preferred_element_type=F32).astype(BF16)
        out[0, :, 512 * j : 512 * j + 512] = res[:128]
        out[1, :, 512 * j : 512 * j + 512] = res[128:]
        block = (slice(None), slice(None), pl.ds(512 * j, 512))
        copies.append(pltpu.make_async_copy(out.at[block], out_h.at[block], sems.at[j]))
        copies[-1].start()
    for copy in copies:
        copy.wait()


def vmem():
    return pl.BlockSpec(memory_space=pltpu.VMEM)


def hbm():
    return pl.BlockSpec(memory_space=pltpu.HBM)


def params(mib):
    return pltpu.CompilerParams(vmem_limit_bytes=mib * MIB)


def cost(flops, size):
    return pl.CostEstimate(flops=flops, bytes_accessed=size, transcendentals=0)


def shards(raw, filt, range_off, fine, dop, pulse_order, band_idx):
    own = pl.pallas_call(
        window_kernel,
        out_shape=jax.ShapeDtypeStruct((16, 8, BW), BF16),
        in_specs=[hbm()] * 6,
        out_specs=vmem(),
        scratch_shapes=[
            pltpu.SMEM((1, 4), jnp.int32),
            pltpu.SMEM((4,), jnp.int32),
            pltpu.SMEM((4,), jnp.int32),
            pltpu.SMEM((4,), jnp.int32),
            pltpu.SMEM((4, 16), jnp.int32),
            pltpu.VMEM((2, 4, UPS), BF16),
            pltpu.SemaphoreType.DMA((6,)),
        ],
        compiler_params=params(60),
    )(pulse_order, range_off, fine, dop, band_idx.T, raw)
    plane = lax.all_to_all(
        own, AXES, split_axis=0, concat_axis=0, axis_index_groups=planes(), tiled=True
    ).reshape(CHUNK, BW)
    chunks = [plane] + [lax.ppermute(plane, AXES, along_last(k)) for k in STEPS[1:]]
    band = jax.ShapeDtypeStruct((CHUNK, BW), BF16)
    three = jax.ShapeDtypeStruct((3 * CHUNK, BW), BF16)
    whole = jax.ShapeDtypeStruct((WIN, BW), BF16)
    effort = cost(2 * CHUNK * UPS * UPS, 8 * MIB)
    scratch = [
        pltpu.VMEM((CHUNK, 2 * WIN), BF16),
        pltpu.VMEM((2048, 128), F32),
        pltpu.VMEM((2, 16 * 72, 128), F32),
        pltpu.VMEM((8, 128), jnp.int32),
        pltpu.SMEM((8, 128), jnp.int32),
        pltpu.SemaphoreType.DMA,
    ]
    first_bands = pl.pallas_call(
        first_band_kernel,
        out_shape=[three, whole, jax.ShapeDtypeStruct(filt.shape, BF16)],
        in_specs=[vmem(), hbm()],
        out_specs=[vmem()] * 3,
        scratch_shapes=scratch + [pltpu.SemaphoreType.DMA((4,))],
        compiler_params=params(FIRST),
        cost_estimate=effort,
    )
    theirs, mine, filt_v = first_bands(chunks[0], filt)
    for index in (1, 2):
        theirs, mine = pl.pallas_call(
            functools.partial(middle_band_kernel, index),
            out_shape=[three, whole],
            in_specs=[vmem()] * 4,
            out_specs=[vmem()] * 2,
            scratch_shapes=scratch,
            input_output_aliases={2: 0, 3: 1},
            compiler_params=params(12),
            cost_estimate=effort,
        )(chunks[index], filt_v, theirs, mine)
    theirs, chunks[3] = lax.optimization_barrier((theirs, chunks[3]))
    given = lax.ppermute(theirs, AXES, other_core())
    theirs, mine = pl.pallas_call(
        last_band_kernel,
        out_shape=[band, whole],
        in_specs=[vmem()] * 3,
        out_specs=[vmem()] * 2,
        scratch_shapes=scratch,
        input_output_aliases={2: 1},
        compiler_params=params(12),
        cost_estimate=effort,
    )(chunks[3], filt_v, mine)
    last = lax.ppermute(theirs, AXES, other_core())
    sums, info, early = pl.pallas_call(
        sum_kernel,
        out_shape=[
            jax.ShapeDtypeStruct((16, BW), F32),
            jax.ShapeDtypeStruct((8, EARLY), F32),
            whole,
        ],
        in_specs=[vmem()] * 2,
        out_specs=[vmem()] * 3,
        input_output_aliases={1: 2},
        compiler_params=params(12),
        cost_estimate=cost(2 * 16 * EARLY * BW, 4 * MIB),
    )(given, mine)
    partial, meta, b = pl.pallas_call(
        gradient_kernel,
        out_shape=[
            jax.ShapeDtypeStruct((16, 8, 128), F32),
            jax.ShapeDtypeStruct((2, 8, 128), F32),
            jax.ShapeDtypeStruct((WIN, BW), BF16),
        ],
        in_specs=[vmem()] * 4,
        out_specs=[vmem()] * 3,
        scratch_shapes=[pltpu.VMEM((8, 128), F32)],
        input_output_aliases={3: 2},
        compiler_params=params(12),
    )(last, sums, info, early)
    grads = lax.all_to_all(partial, "tile", split_axis=0, concat_axis=0, tiled=True)
    return pl.pallas_call(
        image_kernel,
        out_shape=jax.ShapeDtypeStruct((2, ROWS, 4 * WIN), BF16),
        in_specs=[vmem()] * 3,
        out_specs=hbm(),
        scratch_shapes=[
            pltpu.VMEM((8, 128), F32),
            pltpu.VMEM((512, WIN), BF16),
            pltpu.VMEM((256, 2 * WIN), BF16),
            pltpu.VMEM((2, ROWS, 4 * WIN), BF16),
            pltpu.SemaphoreType.DMA((8,)),
        ],
        compiler_params=params(20),
    )(grads, meta, b)


def solution(mesh):
    return jax.shard_map(
        shards,
        mesh=mesh,
        in_specs=(
            P(None, AXES, None),
            P(),
            P(AXES),
            P(AXES),
            P(AXES),
            P(AXES, None),
            P(None, AXES),
        ),
        out_specs=P(None, "pulse", "tile"),
        check_vma=False,
    )
```

```python
import functools

import jax
import jax.numpy as jnp
from jax import lax
from jax.experimental import pallas as pl
from jax.experimental.pallas import tpu as pltpu
from jax.sharding import PartitionSpec as P

AXES = ("pulse", "tile")
WIN = 1024
UPS = 2048
BW = WIN + 128
ROWS = 128
CHUNK = 128
EARLY = 7 * CHUNK
STEPS = (0, 1, 3, 2)
F32 = jnp.float32
BF16 = jnp.bfloat16
NT = (((1,), (1,)), ((), ()))
MIB = 1024 * 1024
FIRST = 42


def linear(z, y, x, core):
    return (z * 2 + y % 2) * 16 + ((y // 2) * 4 + x) * 2 + core


PLACES = [(z, y, x, c) for z in range(4) for y in range(4) for x in range(4) for c in range(2)]


def planes():
    groups = {}
    for z, y, x, c in PLACES:
        groups.setdefault((c, x if c == 0 else y), []).append(linear(z, y, x, c))
    return [groups[key] for key in sorted(groups)]


def along_last(k):
    return [
        (
            linear(z, y, x, c),
            linear(z, y, (x + k) % 4, c) if c == 0 else linear(z, (y + k) % 4, x, c),
        )
        for z, y, x, c in PLACES
    ]


def other_core():
    return [(linear(z, y, x, c), linear(z, y, x, 1 - c)) for z, y, x, c in PLACES]


def pairs(partner):
    return [(linear(*place), linear(*partner(*place))) for place in PLACES]


def iota(shape, axis):
    return lax.broadcasted_iota(jnp.int32, shape, axis)


def window_kernel(order_h, off_h, fine_h, dop_h, band_h, raw_h, out, order, off, fine, dop, band, raw, sems):
    pairs = ((order_h, order), (off_h, off), (fine_h, fine), (dop_h, dop), (band_h, band), (raw_h, raw))
    copies = [pltpu.make_async_copy(a, b, sems.at[i]) for i, (a, b) in enumerate(pairs)]
    for copy in copies:
        copy.start()
    for copy in copies:
        copy.wait()
    x = jnp.concatenate([raw[0].astype(F32), raw[1].astype(F32)], 0)
    row = iota((8, WIN), 0)
    lane = iota((1, 128), 1)
    meta_row = iota((8, 128), 0)
    both = jnp.zeros((8, WIN), F32)
    meta = jnp.zeros((8, 128), jnp.int32)
    for j in range(4):
        k = order[0, j]
        y = pltpu.roll(x, lax.rem(UPS - off[k], UPS), 1)[:, :WIN]
        one_re = jnp.sum(jnp.where(row == k, y, 0.0), axis=0, keepdims=True)
        one_im = jnp.sum(jnp.where(row == k + 4, y, 0.0), axis=0, keepdims=True)
        both = jnp.where(row == j, one_re, jnp.where(row == j + 4, one_im, both))
        d = dop[k]
        v = jnp.where(lane == 1, fine[k], 0)
        v = jnp.where(lane == 2, d >> 5, v)
        v = jnp.where(lane == 3, d & 31, v)
        for t in range(16):
            b = band[k, t]
            v = jnp.where(lane == 16 + t, b >> 5, v)
            v = jnp.where(lane == 32 + t, b & 31, v)
        meta = jnp.where((meta_row & 3) == j, v, meta)
    both = both.astype(BF16)
    meta = meta.astype(F32).astype(BF16)
    for i in range(16):
        out[i, :, :WIN] = both
        out[i, :, WIN:] = meta


def first_band_kernel(m, filt_h, theirs, mine, filt, w, prof, cut, starts_v, starts_s, sem, sems):
    copies = []
    for i in range(4):
        block = (slice(None), slice(None), pl.ds(512 * i, 512))
        copies.append(pltpu.make_async_copy(filt_h.at[block], filt.at[block], sems.at[i]))
        copies[-1].start()
    outs = (theirs, 0, mine, 0)
    cut_bands(m, filt, outs, (w, prof, cut, starts_v, starts_s, sem), copies)


def middle_band_kernel(index, m, filt, theirs_in, mine_in, theirs, mine, *scratch):
    cut_bands(m, filt, (theirs, CHUNK * index, mine, CHUNK * index), scratch)


def last_band_kernel(m, filt, mine_in, theirs, mine, *scratch):
    cut_bands(m, filt, (theirs, 0, mine, CHUNK * 3), scratch)


def cut_bands(m, filt, outs, scratch, copies=None):
    theirs, theirs_at, mine, mine_at = outs
    w, prof, cut, starts_v, starts_s, sem = scratch
    tile = lax.axis_index("tile")
    sibling = tile + 1 - 2 * lax.rem(tile, 2)
    lane8 = iota((8, 128), 1)
    row8 = iota((8, 128), 0)
    info = m[:, WIN:]
    want = jnp.where(row8 == 0, tile, sibling)
    pick = jnp.where(lane8 == want + 16, 32.0, jnp.where(lane8 == want + 32, 1.0, 0.0)).astype(BF16)
    starts_v[...] = lax.dot_general(pick, info, NT, preferred_element_type=F32).astype(jnp.int32)
    copy = pltpu.make_async_copy(starts_v, starts_s, sem)
    copy.start()
    k = iota((128, 256), 0)
    want = jnp.where(iota((128, 256), 1) < 128, tile, sibling)
    spread = jnp.where(k == want + 16, 32.0, jnp.where(k == want + 32, 1.0, 0.0)).astype(BF16)
    turns = jnp.dot(info, spread, preferred_element_type=F32).astype(jnp.int32) & 127

    sign = jnp.where(iota((8, WIN), 0) < 4, -1.0, 1.0)
    w[:, :WIN] = m[:, :WIN]
    for g in range(0, CHUNK, 16):
        v = m[g : g + 16, :WIN].astype(F32)
        top = pltpu.roll(v[:8], 4, 0) * sign
        low = pltpu.roll(v[8:], 4, 0) * sign
        w[g : g + 16, WIN:] = jnp.concatenate([top, low], 0).astype(BF16)
    for n in range(0, UPS, 512):
        if copies:
            copies[n // 512].wait()
        f = filt[:, :, n : n + 512].reshape(2 * WIN, 512)
        r = jnp.dot(w[...], f, preferred_element_type=F32)
        for h in range(4):
            for g in range(16):
                at = g * 128 + (n // 128 + h) * 8
                prof[at : at + 8, :] = r[8 * g : 8 * g + 8, 128 * h : 128 * h + 128]
    copy.wait()
    for which in range(2):
        for g in range(16):
            for j in range(4):
                start = starts_s[1 - which, 8 * g + j]
                turn = (128 - (start & 127)) & 127
                at = g * 128 + (start >> 7) * 8 + j
                re = pltpu.roll(prof[pl.ds(at, 8, 8), :], turn, 1)
                im = pltpu.roll(prof[pl.ds(at + 4, 8, 8), :], turn, 1)
                end = pltpu.roll(prof[pl.ds(at + 64, 2, 4), :], turn, 1)
                to = g * 72 + j
                cut[which, pl.ds(to, 8, 8), :] = re
                cut[which, pl.ds(to + 4, 8, 8), :] = im
                cut[which, pl.ds(to + 64, 2, 4), :] = end
    for which, (out, to) in enumerate(((theirs, theirs_at), (mine, mine_at))):
        for pair in range(8):
            done = [[], []]
            for e in range(2):
                g = 2 * pair + e
                turn = turns[8 * g : 8 * g + 8, 128 * (1 - which) : 128 * (1 - which) + 128]
                inside = lane8 + turn < 128
                parts = [cut[which, g * 72 + 8 * c : g * 72 + 8 * c + 8, :] for c in range(9)]
                done[e] = [jnp.where(inside, parts[c], parts[c + 1]) for c in range(8)]
                meta = info[8 * g : 8 * g + 8].astype(F32)
                done[e].append(
                    jnp.where(lane8 == 0, parts[8], jnp.where(lane8 < 4, meta, 0.0))
                )
            for c in range(9):
                v = jnp.concatenate([done[0][c], done[1][c]], 0).astype(BF16)
                at = to + 16 * pair
                out[at : at + 16, 128 * c : 128 * c + 128] = v


def positions():
    tile = lax.axis_index("tile")
    core = lax.rem(tile, 2)
    x = lax.rem(tile // 2, 4)
    y = tile // 8 * 2 + lax.rem(lax.axis_index("pulse"), 2)
    own = jnp.where(core == 0, x, y)
    other = jnp.where(core == 0, y, x)
    return [core * 4 + lax.rem(own + 4 - k, 4) for k in STEPS] + [
        (1 - core) * 4 + lax.rem(other + 4 - k, 4) for k in STEPS
    ]


def lane_info(b):
    row8 = iota((8, 128), 0)
    lane8 = iota((8, 128), 1)
    pick = jnp.where(
        row8 == 0,
        jnp.where(lane8 == 1, 1.0, 0.0),
        jnp.where(row8 == 1, jnp.where(lane8 == 2, 32.0, jnp.where(lane8 == 3, 1.0, 0.0)), 0.0),
    ).astype(BF16)
    return lax.dot_general(pick, b, NT, preferred_element_type=F32)


def block_rows(shift):
    size = shift.shape[1]
    keep = jnp.where((iota((8, size), 1) & 7) == iota((8, size), 0), 1.0, 0.0)
    return jnp.concatenate([keep, keep * shift], 0).astype(BF16)


def sum_kernel(given, b_in, sums, info, b):
    b[4 * CHUNK : EARLY, :] = given[...]
    halves = ((b_in, 0, 4 * CHUNK), (given, 4 * CHUNK, EARLY))
    for part, low, high in halves:
        info[:, low:high] = lane_info(part[: high - low, WIN:])
    total = jnp.zeros((16, BW), F32)
    for part, low, high in halves:
        lhs = block_rows(info[0:1, low:high] * 0.0625)
        total += jnp.dot(lhs, part[: high - low], preferred_element_type=F32)
    sums[...] = total


def gradient_kernel(last, early, info, b_in, g_out, meta_out, b):
    b[EARLY:, :] = last[...]
    late = lane_info(last[:, WIN:])
    meta = jnp.concatenate([info[0:2], late[0:2]], 1)
    for i in range(8):
        for e in range(2):
            meta_out[e, i : i + 1, :] = meta[e : e + 1, CHUNK * i : CHUNK * (i + 1)]
    shift = meta[0:1] * 0.0625
    sums = early[...] + jnp.dot(block_rows(late[0:1] * 0.0625), last[...], preferred_element_type=F32)
    s = sums[:8]
    t = sums[8:]
    inner = iota((8, BW), 1) < WIN
    x0 = s + pltpu.roll(t, BW - 1, 1) - t
    dr = pltpu.roll(s, BW - 1, 1) - s
    a = jnp.where(inner, 4.0 * x0 + 1.5 * dr, 0.0)
    d = jnp.where(inner, 1.5 * x0 + 0.875 * dr, 0.0)
    p = a - d + pltpu.roll(d, 1, 1)
    q = pltpu.roll(a, 1, 1) - a
    both = jnp.concatenate([p, q], 0)
    high = both.astype(BF16)
    low = (both - high.astype(F32)).astype(BF16)
    lhs = jnp.concatenate([high, low], 0)
    g = jnp.concatenate(
        [
            lax.dot_general(lhs, b_in[:EARLY], NT, preferred_element_type=F32),
            lax.dot_general(lhs, last[...], NT, preferred_element_type=F32),
        ],
        1,
    )
    g = g[:16] + g[16:]
    g = g[:8] + g[8:] * shift
    j = iota((8, WIN), 1) & 3
    row = iota((8, WIN), 0)
    by_re = jnp.sum(jnp.where(row == j, g, 0.0), axis=0, keepdims=True)
    by_im = jnp.sum(jnp.where(row == j + 4, g, 0.0), axis=0, keepdims=True)
    even = (iota((1, WIN), 1) & 4) == 0
    swapped = jnp.where(even, pltpu.roll(by_im, WIN - 4, 1), -pltpu.roll(by_im, 4, 1))
    grads = by_re + swapped
    for i, at in enumerate(positions()):
        g_out[pl.ds(at, 1), :] = grads[:, CHUNK * i : CHUNK * (i + 1)]


def turn(m):
    quadrant = (m + 128) >> 8
    p = (m - (quadrant << 8)).astype(F32) * (2.0 * jnp.pi / 1024.0)
    p2 = p * p
    c = 1.0 + p2 * (-1.0 / 2 + p2 * (1.0 / 24 + p2 * (-1.0 / 720 + p2 * (1.0 / 40320))))
    s = p * (1.0 + p2 * (-1.0 / 6 + p2 * (1.0 / 120 + p2 * (-1.0 / 5040 + p2 * (1.0 / 362880)))))
    odd = (quadrant & 1) == 1
    cos = jnp.where(odd, s, c)
    sin = jnp.where(odd, c, s)
    cos = jnp.where(((quadrant + 1) & 2) == 2, -cos, cos)
    sin = jnp.where((quadrant & 2) == 2, -sin, sin)
    return cos, sin


def image_kernel(g_in, g_other, meta, b, out_h, total, lhs, xd, out, sems):
    total[...] = g_in[...] + g_other[...]
    even8 = (iota((8, 128), 1) & 4) == 0
    local = jnp.concatenate([total[pl.ds(at, 1), :] for at in positions()], 0)
    g_re = jnp.where(even8, local, pltpu.roll(local, 4, 1))
    g_im = jnp.where(even8, pltpu.roll(local, 124, 1), local)
    inv = (512.0**-0.5) / jnp.sqrt(g_re * g_re + g_im * g_im + 1.0)
    c_re = jnp.where(even8, g_re, g_im) * inv
    c_im = jnp.where(even8, -g_im, g_re) * inv

    def wide(v):
        return jnp.concatenate([v[i : i + 1] for i in range(8)], 1)

    shift = wide(meta[0]) * 0.0625
    dop = wide(meta[1].astype(jnp.int32))
    c_re = wide(c_re)
    c_im = wide(c_im)
    pulse = lax.axis_index("pulse")
    cu, su = turn(((iota((16, WIN), 0) * 8 + pulse * ROWS) * dop) & 1023)
    cv, sv = turn((iota((8, WIN), 0) * dop) & 1023)
    vr = cv * c_re - sv * c_im
    vi = cv * c_im + sv * c_re
    for u in range(0, 16, 2):
        pair = []
        for e in range(2):
            ur = cu[u + e : u + e + 1]
            ui = su[u + e : u + e + 1]
            pair.append((ur * vr - ui * vi, ur * vi + ui * vr))
        at = 8 * u
        for z in range(2):
            v = jnp.concatenate([pair[0][z], pair[1][z]], 0)
            lhs[at + 128 * z : at + 128 * z + 16, :] = v.astype(BF16)
            lhs[at + 256 + 128 * z : at + 272 + 128 * z, :] = (v * shift).astype(BF16)
    uv = jnp.dot(lhs[...], b[...], preferred_element_type=F32)
    diff = pltpu.roll(uv, BW - 1, 1) - uv
    xd[:, :WIN] = (uv[:256] + diff[256:])[:, :WIN].astype(BF16)
    xd[:, WIN:] = diff[:256, :WIN].astype(BF16)
    k = iota((256, 512), 0)
    col = iota((256, 512), 1)
    quarter = (col & 3).astype(F32) * 0.25
    spread = jnp.where((k & 127) == (col >> 2), jnp.where(k < 128, 1.0, quarter), 0.0).astype(BF16)
    copies = []
    for j in range(8):
        at = 128 * j
        part = jnp.concatenate([xd[:, at : at + 128], xd[:, WIN + at : WIN + at + 128]], 1)
        res = jnp.dot(part, spread, preferred_element_type=F32).astype(BF16)
        out[0, :, 512 * j : 512 * j + 512] = res[:128]
        out[1, :, 512 * j : 512 * j + 512] = res[128:]
        block = (slice(None), slice(None), pl.ds(512 * j, 512))
        copies.append(pltpu.make_async_copy(out.at[block], out_h.at[block], sems.at[j]))
        copies[-1].start()
    for copy in copies:
        copy.wait()


def vmem():
    return pl.BlockSpec(memory_space=pltpu.VMEM)


def hbm():
    return pl.BlockSpec(memory_space=pltpu.HBM)


def params(mib):
    return pltpu.CompilerParams(vmem_limit_bytes=mib * MIB)


def cost(flops, size):
    return pl.CostEstimate(flops=flops, bytes_accessed=size, transcendentals=0)


def shards(raw, filt, range_off, fine, dop, pulse_order, band_idx):
    own = pl.pallas_call(
        window_kernel,
        out_shape=jax.ShapeDtypeStruct((16, 8, BW), BF16),
        in_specs=[hbm()] * 6,
        out_specs=vmem(),
        scratch_shapes=[
            pltpu.SMEM((1, 4), jnp.int32),
            pltpu.SMEM((4,), jnp.int32),
            pltpu.SMEM((4,), jnp.int32),
            pltpu.SMEM((4,), jnp.int32),
            pltpu.SMEM((4, 16), jnp.int32),
            pltpu.VMEM((2, 4, UPS), BF16),
            pltpu.SemaphoreType.DMA((6,)),
        ],
        compiler_params=params(60),
    )(pulse_order, range_off, fine, dop, band_idx.T, raw)
    plane = lax.all_to_all(
        own, AXES, split_axis=0, concat_axis=0, axis_index_groups=planes(), tiled=True
    ).reshape(CHUNK, BW)
    chunks = [plane] + [lax.ppermute(plane, AXES, along_last(k)) for k in STEPS[1:]]
    band = jax.ShapeDtypeStruct((CHUNK, BW), BF16)
    three = jax.ShapeDtypeStruct((3 * CHUNK, BW), BF16)
    whole = jax.ShapeDtypeStruct((WIN, BW), BF16)
    effort = cost(2 * CHUNK * UPS * UPS, 8 * MIB)
    scratch = [
        pltpu.VMEM((CHUNK, 2 * WIN), BF16),
        pltpu.VMEM((2048, 128), F32),
        pltpu.VMEM((2, 16 * 72, 128), F32),
        pltpu.VMEM((8, 128), jnp.int32),
        pltpu.SMEM((8, 128), jnp.int32),
        pltpu.SemaphoreType.DMA,
    ]
    first_bands = pl.pallas_call(
        first_band_kernel,
        out_shape=[three, whole, jax.ShapeDtypeStruct(filt.shape, BF16)],
        in_specs=[vmem(), hbm()],
        out_specs=[vmem()] * 3,
        scratch_shapes=scratch + [pltpu.SemaphoreType.DMA((4,))],
        compiler_params=params(FIRST),
        cost_estimate=effort,
    )
    theirs, mine, filt_v = first_bands(chunks[0], filt)
    for index in (1, 2):
        theirs, mine = pl.pallas_call(
            functools.partial(middle_band_kernel, index),
            out_shape=[three, whole],
            in_specs=[vmem()] * 4,
            out_specs=[vmem()] * 2,
            scratch_shapes=scratch,
            input_output_aliases={2: 0, 3: 1},
            compiler_params=params(12),
            cost_estimate=effort,
        )(chunks[index], filt_v, theirs, mine)
    theirs, chunks[3] = lax.optimization_barrier((theirs, chunks[3]))
    given = lax.ppermute(theirs, AXES, other_core())
    theirs, mine = pl.pallas_call(
        last_band_kernel,
        out_shape=[band, whole],
        in_specs=[vmem()] * 3,
        out_specs=[vmem()] * 2,
        scratch_shapes=scratch,
        input_output_aliases={2: 1},
        compiler_params=params(12),
        cost_estimate=effort,
    )(chunks[3], filt_v, mine)
    last = lax.ppermute(theirs, AXES, other_core())
    sums, info, early = pl.pallas_call(
        sum_kernel,
        out_shape=[
            jax.ShapeDtypeStruct((16, BW), F32),
            jax.ShapeDtypeStruct((8, EARLY), F32),
            whole,
        ],
        in_specs=[vmem()] * 2,
        out_specs=[vmem()] * 3,
        input_output_aliases={1: 2},
        compiler_params=params(12),
        cost_estimate=cost(2 * 16 * EARLY * BW, 4 * MIB),
    )(given, mine)
    partial, meta, b = pl.pallas_call(
        gradient_kernel,
        out_shape=[
            jax.ShapeDtypeStruct((8, 128), F32),
            jax.ShapeDtypeStruct((2, 8, 128), F32),
            jax.ShapeDtypeStruct((WIN, BW), BF16),
        ],
        in_specs=[vmem()] * 4,
        out_specs=[vmem()] * 3,
        input_output_aliases={3: 2},
        compiler_params=params(12),
    )(last, sums, info, early)
    for partner in (
        other_core(),
        pairs(lambda z, y, x, c: (z, y, x ^ 1, c)),
        pairs(lambda z, y, x, c: (z, y, x ^ 3, c)),
    ):
        partial = partial + lax.ppermute(partial, AXES, partner)
    others = lax.ppermute(partial, AXES, pairs(lambda z, y, x, c: (z, 3 - y, x, c)))
    return pl.pallas_call(
        image_kernel,
        out_shape=jax.ShapeDtypeStruct((2, ROWS, 4 * WIN), BF16),
        in_specs=[vmem()] * 4,
        out_specs=hbm(),
        scratch_shapes=[
            pltpu.VMEM((8, 128), F32),
            pltpu.VMEM((512, WIN), BF16),
            pltpu.VMEM((256, 2 * WIN), BF16),
            pltpu.VMEM((2, ROWS, 4 * WIN), BF16),
            pltpu.SemaphoreType.DMA((8,)),
        ],
        compiler_params=params(20),
    )(partial, others, meta, b)


def solution(mesh):
    return jax.shard_map(
        shards,
        mesh=mesh,
        in_specs=(
            P(None, AXES, None),
            P(),
            P(AXES),
            P(AXES),
            P(AXES),
            P(AXES, None),
            P(None, AXES),
        ),
        out_specs=P(None, "pulse", "tile"),
        check_vma=False,
    )
```
